32 devices in a mesh: seq: 16 (over z, y, x), tensor: 2 (over core).
Axes of the slice: x: 2, y: 2, z: 4, core: 2. Of those that a mesh axis runs over, the one named last changes fastest.
Arguments:
- hidden_in: bfloat16 [2048, 2560], P('seq', 'tensor'), may hold values from -6 to 6
- norm_gain: float32 [2560], replicated, may hold values from 0.1 to 1.9
- w_query: bfloat16 [2560, 2048], P(None, 'tensor'), may hold values from -0.125 to 0.125
- w_key: bfloat16 [2560, 1024], P(None, 'tensor'), may hold values from -0.125 to 0.125
- w_value: bfloat16 [2560, 1024], P(None, 'tensor'), may hold values from -0.125 to 0.125
- w_out: bfloat16 [2048, 2560], P('tensor'), may hold values from -0.125 to 0.125
- q_gain: float32 [128], replicated, may hold values from 0.1 to 1.9
- k_gain: float32 [128], replicated, may hold values from 0.1 to 1.9
- lengths: int32 [16], replicated, may hold values from 1 to 1536, 2048 in all
Outputs:
- attn_out: bfloat16 [2048, 2560], P(('seq', 'tensor'))
- key_cache: bfloat16 [2048, 1024], P('seq', 'tensor')
- value_cache: bfloat16 [2048, 1024], P('seq', 'tensor')
The draws below stay inside these ranges and needn't reach their ends.
Inputs may be any that keep to these rules, and one draw needn't show every extreme that they name: The lengths sum to 2048 and the largest is exactly 1536.
All inputs are finite; a program needn't handle non-finite values.
Results may differ from the reference program's by a relative error of at most 0.015.
Values may be sent and summed in bfloat16 or wider, within the bound.
A program may use at most 64 MiB of HBM per device.

```python
import math
import jax
import jax.numpy as jnp
import numpy as np
from jax import lax

D = 2560
HD = 128
KVH = 8
QH = 16
NSEG = 16
TOKENS = 2048
MAXLEN = 1536


def steps_of(rng, shape, cuts, least, largest):
    factor_of = 1.0
    for axis_at, parts in cuts:
        steps = jax.random.uniform(jax.random.fold_in(jax.random.fold_in(rng, 6), axis_at), (parts,), jnp.float32, least / len(cuts), largest / len(cuts))
        factor_of = factor_of * jnp.repeat(jnp.exp(steps), shape[axis_at] // parts).reshape((-1,) + (1,) * (len(shape) - 1 - axis_at))
    return factor_of


def length_profile(number_of, total, reach, skew):
    loads = [(1 << 20) // math.isqrt(standing ** skew) + 1 for standing in range(2, number_of + 1)]
    surplus, given = total - reach - (number_of - 1), [1] * (number_of - 1)
    while surplus > 0:
        candidates = [i for i in range(number_of - 1) if given[i] < reach]
        pool, left = sum([loads[i] for i in candidates]), surplus
        for i in candidates:
            more = min(reach - given[i], max(1, left * loads[i] // pool), surplus)
            given[i] = given[i] + more
            surplus = surplus - more
    return np.array([reach] + given)


def uneven_parts(rng, amount, total, limit, slope):
    if amount == 2:
        one = jax.random.randint(rng, (), max(1, total - limit), min(limit, total - 1) + 1)
        return jnp.stack([one, total - one])
    sizes = jnp.asarray(length_profile(amount, total, limit, slope), jnp.int32)
    pairs = (amount - 1) // 2
    source_of, taker = sizes[1:1 + 2 * pairs:2], sizes[2:2 + 2 * pairs:2]
    margin = jnp.minimum(source_of - 1, limit - taker)
    passed = jax.random.randint(jax.random.fold_in(rng, 1), (pairs,), 0, 1 << 20) % (margin + 1)
    sizes = sizes.at[1:1 + 2 * pairs:2].set(source_of - passed).at[2:2 + 2 * pairs:2].set(taker + passed)
    return sizes[jax.random.permutation(jax.random.fold_in(rng, 2), amount)]


def bell_draw(key, extent, scale, bound, pieces=(), kind=jnp.bfloat16):
    drawn = jax.random.normal(key, extent, jnp.float32) * scale
    if len(pieces) > 0:
        drawn = steps_of(key, extent, pieces, -0.22, 0.18) * drawn
    return jnp.clip(drawn, min=-bound, max=bound).astype(kind)


def setup_inputs(seed: int = 0) -> dict:
    key_list = jax.random.split(jax.random.key(seed), 10)
    hidden_in = bell_draw(key_list[0], (TOKENS, D), 1.0, 6.0, ((0, 16), (1, 2)))
    norm_gain = jnp.clip(1.0 + 0.18 * jax.random.normal(key_list[1], (D,), jnp.float32), 0.1, 1.9)
    w_query = bell_draw(key_list[2], (D, QH * HD), D ** -0.5, 0.125, ((1, 2),))
    w_key = bell_draw(key_list[3], (D, KVH * HD), D ** -0.5, 0.125, ((1, 2),))
    w_value = bell_draw(key_list[4], (D, KVH * HD), D ** -0.5, 0.125, ((1, 2),))
    w_out = bell_draw(key_list[5], (QH * HD, D), (QH * HD) ** -0.5, 0.125, ((0, 2),))
    q_gain = jnp.clip(1.0 + 0.18 * jax.random.normal(key_list[6], (HD,), jnp.float32), 0.1, 1.9)
    k_gain = jnp.clip(1.0 + 0.18 * jax.random.normal(key_list[7], (HD,), jnp.float32), 0.1, 1.9)
    lengths = uneven_parts(key_list[8], NSEG, TOKENS, MAXLEN, 2).astype(jnp.int32)
    return {"hidden_in": hidden_in, "norm_gain": norm_gain, "w_query": w_query, "w_key": w_key, "w_value": w_value, "w_out": w_out, "q_gain": q_gain, "k_gain": k_gain, "lengths": lengths}


rope_base = 1000000.0
norm_eps = 1e-06
masked = -1e+30

def prompt_starts(lengths, token_pos):
    ends = jnp.cumsum(lengths)
    starts = ends - lengths
    before = (ends[None, :] <= token_pos[:, None]).astype(jnp.int32)
    segment = lax.optimization_barrier(jnp.sum(before, axis=1))
    onehot = segment[:, None] == jnp.arange(lengths.shape[0], dtype=jnp.int32)[None, :]
    return lax.optimization_barrier(jnp.sum(jnp.where(onehot, starts[None, :], 0), axis=1)).astype(jnp.int32)

def head_norm_rope(values, gain, rel_pos):
    width = values.shape[-1]
    half = width // 2
    mean_sq = lax.optimization_barrier(jnp.mean(values * values, axis=-1, keepdims=True))
    normed = values * lax.rsqrt(mean_sq + norm_eps) * gain
    freq = rope_base ** (-jnp.arange(half, dtype=jnp.float32) * 2.0 / width)
    angle = rel_pos.astype(jnp.float32)[:, None] * freq[None, :]
    cosine = jnp.cos(angle)[:, None, :]
    sine = jnp.sin(angle)[:, None, :]
    first = normed[..., :half]
    second = normed[..., half:]
    return jnp.concatenate([first * cosine - second * sine, second * cosine + first * sine], axis=-1)

def reference(hidden_in, norm_gain, w_query, w_key, w_value, w_out, q_gain, k_gain, lengths):
    count = hidden_in.shape[0]
    width = hidden_in.shape[1]
    head_dim = q_gain.shape[0]
    q_heads = w_query.shape[1] // head_dim
    kv_heads = w_key.shape[1] // head_dim
    group = q_heads // kv_heads
    token_pos = jnp.arange(count, dtype=jnp.int32)
    seg_start = prompt_starts(lengths, token_pos)
    rel_pos = token_pos - seg_start
    wide = hidden_in.astype(jnp.float32)
    scaled = (wide * norm_gain[None, :]).astype(jnp.bfloat16)
    inv_rms = lax.rsqrt(lax.optimization_barrier(jnp.sum(wide * wide, axis=1)) / width + norm_eps)[:, None]
    q_raw = jnp.dot(scaled, w_query, preferred_element_type=jnp.float32) * inv_rms
    k_raw = jnp.dot(scaled, w_key, preferred_element_type=jnp.float32) * inv_rms
    value_cache = (jnp.dot(scaled, w_value, preferred_element_type=jnp.float32) * inv_rms).astype(jnp.bfloat16)
    queries = head_norm_rope(q_raw.reshape(count, q_heads, head_dim), q_gain, rel_pos).astype(jnp.bfloat16)
    keys = head_norm_rope(k_raw.reshape(count, kv_heads, head_dim), k_gain, rel_pos).astype(jnp.bfloat16)
    key_cache = keys.reshape(count, kv_heads * head_dim)
    query_grid = jnp.transpose(queries.reshape(count, kv_heads, group, head_dim), (1, 0, 2, 3))
    key_grid = jnp.transpose(keys, (1, 0, 2))
    value_grid = jnp.transpose(value_cache.reshape(count, kv_heads, head_dim), (1, 0, 2))
    block = math.gcd(count, 512)
    blocks = count // block
    inv_root = 1.0 / math.sqrt(head_dim)

    def one_head(operands):
        q_head, k_head, v_head = operands
        k_wide = k_head.astype(jnp.float32)
        v_wide = v_head.astype(jnp.float32)

        def one_block(index):
            first = (index * block).astype(jnp.int32)
            q_block = lax.dynamic_slice_in_dim(q_head, first, block, 0).astype(jnp.float32)
            q_pos = first + jnp.arange(block, dtype=jnp.int32)
            q_start = lax.dynamic_slice_in_dim(seg_start, first, block, 0)
            score = jnp.einsum('qgd,kd->gqk', q_block, k_wide) * inv_root
            visible = (token_pos[None, :] >= q_start[:, None]) & (token_pos[None, :] <= q_pos[:, None])
            score = jnp.where(visible[None], score, masked)
            top = lax.optimization_barrier(jnp.max(score, axis=-1, keepdims=True))
            weights = jnp.where(visible[None], jnp.exp(score - top), 0.0)
            denom = lax.optimization_barrier(jnp.sum(weights, axis=-1))
            rounded = weights.astype(jnp.bfloat16).astype(jnp.float32)
            summed = jnp.einsum('gqk,kd->gqd', rounded, v_wide)
            return summed / denom[..., None]
        return lax.map(one_block, jnp.arange(blocks, dtype=jnp.int32))
    result = lax.map(one_head, (query_grid, key_grid, value_grid))
    attn = jnp.transpose(result, (1, 3, 0, 2, 4)).reshape(count, q_heads * head_dim).astype(jnp.bfloat16)
    attn_out = jnp.dot(attn, w_out, preferred_element_type=jnp.float32).astype(jnp.bfloat16)
    return (attn_out, key_cache, value_cache)
```

```python
import functools
import math

import jax
import jax.numpy as jnp
import numpy as np
from jax import lax
from jax.experimental import pallas as pl
from jax.experimental.pallas import tpu as pltpu
from jax.sharding import PartitionSpec as P

rope_base = 1000000.0
norm_eps = 1e-06
masked = -1e30


def prompt_starts(lengths, token_pos):
    ends = jnp.cumsum(lengths)
    starts = ends - lengths
    before = (ends[None, :] <= token_pos[:, None]).astype(jnp.int32)
    segment = jnp.sum(before, axis=1)
    onehot = segment[:, None] == jnp.arange(lengths.shape[0], dtype=jnp.int32)[None, :]
    return jnp.sum(jnp.where(onehot, starts[None, :], 0), axis=1)


def head_norm_rope(values, gain, rel_pos):
    width = values.shape[-1]
    half = width // 2
    mean_sq = jnp.mean(values * values, axis=-1, keepdims=True)
    normed = values * lax.rsqrt(mean_sq + norm_eps) * gain
    freq = rope_base ** (-jnp.arange(half, dtype=jnp.float32) * 2.0 / width)
    angle = rel_pos.astype(jnp.float32)[:, None] * freq[None, :]
    cosine = jnp.cos(angle)[:, None, :]
    sine = jnp.sin(angle)[:, None, :]
    first = normed[..., :half]
    second = normed[..., half:]
    return jnp.concatenate(
        [first * cosine - second * sine, second * cosine + first * sine], axis=-1
    )


def on_device(hidden_in, norm_gain, w_query, w_key, w_value, w_out, q_gain, k_gain, lengths):
    tokens = hidden_in.shape[0]
    width = w_query.shape[0]
    head_dim = q_gain.shape[0]
    q_cols = w_query.shape[1]
    kv_cols = w_key.shape[1]
    kv_local = kv_cols // head_dim
    group = q_cols // kv_cols
    combined = jnp.concatenate([w_query, w_key, w_value], axis=1)
    piece = lax.all_gather(hidden_in, "tensor", axis=1, tiled=True)
    wide = piece.astype(jnp.float32)
    rows = combined
    scaled = (wide * norm_gain[None, :]).astype(jnp.bfloat16)
    acc = jnp.dot(scaled, rows, preferred_element_type=jnp.float32)
    acc, sumsq = (acc, jnp.sum(wide * wide, axis=1))
    proj = acc * lax.rsqrt(sumsq / width + norm_eps)[:, None]
    block_index = lax.axis_index("seq")
    token_pos = block_index * tokens + jnp.arange(tokens, dtype=jnp.int32)
    seg_start = prompt_starts(lengths, token_pos)
    rel_pos = token_pos - seg_start
    queries = head_norm_rope(
        proj[:, :q_cols].reshape(tokens, kv_local * group, head_dim), q_gain, rel_pos
    ).astype(jnp.bfloat16)
    keys = head_norm_rope(
        proj[:, q_cols : q_cols + kv_cols].reshape(tokens, kv_local, head_dim), k_gain, rel_pos
    ).astype(jnp.bfloat16)
    key_flat = keys.reshape(tokens, kv_cols)
    value_flat = proj[:, q_cols + kv_cols :].astype(jnp.bfloat16)
    query_grid = queries.reshape(tokens, kv_local, group, head_dim)
    inv_root = 1.0 / math.sqrt(head_dim)
    last_pos = jnp.max(token_pos)
    first_start = jnp.min(seg_start)

    def attend_block(carry, key_block, value_block, key_start):
        rows = key_block.shape[0]
        key_pos = key_start + jnp.arange(rows, dtype=jnp.int32)

        def compute(state):
            best, total, summed = state
            key_heads = key_block.reshape(rows, kv_local, head_dim)
            value_heads = value_block.reshape(rows, kv_local, head_dim)
            score = (
                jnp.einsum(
                    "qhgd,khd->hgqk", query_grid, key_heads, preferred_element_type=jnp.float32
                )
                * inv_root
            )
            visible = (key_pos[None, :] >= seg_start[:, None]) & (
                key_pos[None, :] <= token_pos[:, None]
            )
            score = jnp.where(visible[None, None], score, masked)
            fresh = jnp.maximum(best, jnp.max(score, axis=-1))
            weights = jnp.where(visible[None, None], jnp.exp(score - fresh[..., None]), 0.0)
            decay = jnp.exp(best - fresh)
            total = total * decay + jnp.sum(weights, axis=-1)
            summed = summed * decay[..., None] + jnp.einsum(
                "hgqk,khd->hgqd",
                weights.astype(jnp.bfloat16),
                value_heads,
                preferred_element_type=jnp.float32,
            )
            return (fresh, total, summed)

        seen = (key_start <= last_pos) & (key_start + rows - 1 >= first_start)
        return lax.cond(seen, compute, lambda state: state, carry)

    start_state = (
        jnp.full((kv_local, group, tokens), masked, jnp.float32),
        jnp.zeros((kv_local, group, tokens), jnp.float32),
        jnp.zeros((kv_local, group, tokens, head_dim), jnp.float32),
    )
    key_piece = lax.all_gather(key_flat, "seq", axis=0, tiled=True)
    value_piece = lax.all_gather(value_flat, "seq", axis=0, tiled=True)
    rows = key_piece.shape[0]
    size = math.gcd(rows, 512)
    count = rows // size

    def one_part(state, part):
        key_part, value_part, offset = part
        return (attend_block(state, key_part, value_part, offset), None)

    offsets = jnp.arange(count, dtype=jnp.int32) * size
    parts = (
        key_piece.reshape(count, size, kv_cols),
        value_piece.reshape(count, size, kv_cols),
        offsets,
    )
    state, unused = lax.scan(one_part, start_state, parts)
    best, total, summed = state
    attn = summed / total[..., None]
    attn = jnp.transpose(attn, (2, 0, 1, 3)).reshape(tokens, q_cols).astype(jnp.bfloat16)
    mixed = lax.psum_scatter(
        jnp.dot(attn, w_out, preferred_element_type=jnp.float32).astype(jnp.bfloat16),
        "tensor",
        scatter_dimension=0,
        tiled=True,
    )
    return (mixed, key_flat, value_flat)


GROUP = 4


def fused_kernel(
    hid, gain, wq, wk, wv, wo, q_gain, k_gain, freq, lens,
    out, key_out, value_out,
    peer_hid, wq_v, wk_v, wv_v, wo_v, kv_send, q_send, kv_buf, q_buf, o_send, o_buf,
    seg_q, acc, den, y_send, y_recv, y_mine,
    w_sem, h_sem, kv_ssem, kv_rsem, q_ssem, q_rsem, z_ssem, z_rsem, o_ssem, o_rsem, y_ssem, y_rsem,
):
    f32, bf16 = jnp.float32, jnp.bfloat16
    tok, feat = hid.shape
    seq = lax.axis_index("seq")
    core = lax.axis_index("tensor")
    planes = kv_buf.shape[0] // GROUP
    plane = seq // GROUP
    place = seq % GROUP
    mate = (seq, 1 - core)
    above = (seq + GROUP, core)
    below = (seq - GROUP, core)

    def peer(d):
        return (plane * GROUP + (place + d) % GROUP, core)

    def copy(src, dst, ssem, rsem, device):
        return pltpu.make_async_remote_copy(
            src_ref=src, dst_ref=dst, send_sem=ssem, recv_sem=rsem,
            device_id=device, device_id_type=pl.DeviceIdType.MESH,
        )

    halves = (core, 1 - core)
    loads = {}
    count = 0
    for name, src, dst in (("k", wk, wk_v), ("v", wv, wv_v), ("q", wq, wq_v)):
        for i in range(2):
            loads[name, i] = pltpu.make_async_copy(
                src.at[pl.ds(pl.multiple_of(halves[i] * feat, feat), feat)], dst.at[i], w_sem.at[count]
            )
            count += 1
    for key in (("k", 0), ("v", 0), ("k", 1), ("v", 1), ("q", 0), ("q", 1)):
        loads[key].start()
    load_wo = pltpu.make_async_copy(wo, wo_v, w_sem.at[count])
    load_wo.start()

    barrier = pltpu.get_barrier_semaphore()

    def greet(device):
        pl.semaphore_signal(barrier, inc=1, device_id=device, device_id_type=pl.DeviceIdType.MESH)

    greet(mate)
    for d in range(1, GROUP):
        greet(peer(d))

    @pl.when(plane < planes - 1)
    def _():
        greet(above)

    @pl.when(plane > 0)
    def _():
        greet(below)

    neighbours = (plane + planes - 1) // planes + (2 * planes - 2 - plane) // planes
    pl.semaphore_wait(barrier, GROUP + neighbours)

    hid_copy = copy(hid, peer_hid, h_sem.at[0], h_sem.at[1], mate)
    hid_copy.start()

    lengths = [lens[j] for j in range(lens.shape[0])]
    ends, run = [], jnp.int32(0)
    for length in lengths:
        run = run + length
        ends.append(run)
    for b in range(GROUP):
        pos = lax.broadcasted_iota(jnp.int32, (tok, 128), 0) + (plane * GROUP + b) * tok
        start = jnp.zeros((tok, 128), jnp.int32)
        for length, end in zip(lengths, ends):
            start = start + jnp.where(end <= pos, length, 0)
        seg_q[b] = start
    own_pos = lax.broadcasted_iota(jnp.int32, (tok, 128), 0) + seq * tok
    angle = (own_pos - seg_q[place]).astype(f32) * freq[...]
    cosine = jnp.cos(angle)
    lane = lax.broadcasted_iota(jnp.int32, (tok, 128), 1)
    sine = jnp.where(lane < 64, -jnp.sin(angle), jnp.sin(angle))

    x_own = hid[...].astype(f32)
    scaled_own = (x_own * gain[core]).astype(bf16)
    sum_own = jnp.sum(x_own * x_own, axis=1, keepdims=True)
    hid_copy.wait()
    x_far = peer_hid[...].astype(f32)
    scaled_far = (x_far * gain[1 - core]).astype(bf16)
    sumsq = sum_own + jnp.sum(x_far * x_far, axis=1, keepdims=True)
    inv = lax.rsqrt(sumsq / (2 * feat) + norm_eps)

    def project(w, j):
        cols = slice(j * 256, (j + 1) * 256)
        total = jnp.dot(scaled_own, w[0, :, cols], preferred_element_type=f32)
        total = total + jnp.dot(scaled_far, w[1, :, cols], preferred_element_type=f32)
        return total * inv

    def rope(u, g):
        u = u * lax.rsqrt(jnp.mean(u * u, axis=1, keepdims=True) + norm_eps) * g[...]
        return (u * cosine + pltpu.roll(u, 64, 1) * sine).astype(bf16)

    for name in ("k", "v"):
        for i in range(2):
            loads[name, i].wait()
    for j in range(2):
        keys = project(wk_v, j)
        values = project(wv_v, j).astype(bf16)
        value_out[:, j * 256 : (j + 1) * 256] = values
        for i in range(2):
            head = 2 * j + i
            key = rope(keys[:, i * 128 : (i + 1) * 128], k_gain)
            key_out[:, head * 128 : (head + 1) * 128] = key
            kv_send[head, :, :128] = key
            kv_send[head, :, 128:] = values[:, i * 128 : (i + 1) * 128]

    kv_buf[seq] = kv_send[place]

    def up(k, d):
        slot = kv_buf.at[(plane - k) * GROUP + (place + GROUP - d) % GROUP]
        return copy(slot, slot, z_ssem.at[k, d], z_rsem.at[k, d], above)

    def from_below(k, d):
        slot = kv_buf.at[(plane - 1 - k) * GROUP + (place + GROUP - d) % GROUP]
        return copy(slot, slot, z_ssem.at[k, d], z_rsem.at[k, d], below)

    def send_up(k, d):
        @pl.when(plane < planes - 1)
        def _():
            up(k, d).start()

    kv_copies = {}
    for d in range(1, GROUP):
        kv_copies[d] = copy(
            kv_send.at[(place + d) % GROUP], kv_buf.at[seq], kv_ssem.at[d], kv_rsem.at[d], peer(d)
        )
        kv_copies[d].start()
    send_up(0, 0)

    def kv_arrival(d):
        slot = kv_buf.at[plane * GROUP + (place + GROUP - d) % GROUP]
        return copy(slot, slot, kv_ssem.at[d], kv_rsem.at[d], peer(d))

    for i in range(2):
        loads["q", i].wait()
    for j in range(GROUP):
        pair = project(wq_v, j)
        for i in range(2):
            q_send[j, :, i * 128 : (i + 1) * 128] = rope(pair[:, i * 128 : (i + 1) * 128], q_gain)
        if j >= 1:
            kv_arrival(j).wait_recv()
            send_up(0, j)
    q_copies = {}
    for d in range(1, GROUP):
        q_copies[d] = copy(
            q_send.at[(place + d) % GROUP], q_buf.at[place], q_ssem.at[d], q_rsem.at[d], peer(d)
        )
        q_copies[d].start()
    q_buf[place] = q_send[place]
    for d in range(1, GROUP):
        slot = q_buf.at[(place + GROUP - d) % GROUP]
        copy(slot, slot, q_ssem.at[d], q_rsem.at[d], peer(d)).wait_recv()

    scale = math.log2(math.e) / math.sqrt(128)
    span = GROUP * tok

    def attend(k):
        first = (plane - k) * GROUP
        key_pos = lax.broadcasted_iota(jnp.int32, (tok, span), 1) + first * tok

        def one_block(b, carry):
            keys = kv_buf[pl.ds(first, GROUP), :, :128].reshape(span, 128)
            values = kv_buf[pl.ds(first, GROUP), :, 128:].reshape(span, 128)
            start = jnp.concatenate([seg_q[b]] * (span // 128), axis=1)
            visible = key_pos >= start
            if k == 0:
                q_pos = lax.broadcasted_iota(jnp.int32, (tok, span), 0) + (first + b) * tok
                visible = visible & (key_pos <= q_pos)
            for h in range(2):
                cols = slice(h * 128, (h + 1) * 128)
                score = lax.dot_general(
                    q_buf[b, :, cols], keys, (((1,), (1,)), ((), ())), preferred_element_type=f32
                )
                weights = jnp.where(visible, jnp.exp2(score * scale), 0.0)
                part = weights[:, :128]
                for i in range(1, span // 128):
                    part = part + weights[:, i * 128 : (i + 1) * 128]
                summed = jnp.dot(weights.astype(bf16), values, preferred_element_type=f32)
                if k == 0:
                    den[b, :, cols] = part
                    acc[b, :, cols] = summed
                else:
                    den[b, :, cols] += part
                    acc[b, :, cols] += summed
            return carry

        lax.fori_loop(0, GROUP, one_block, 0)

    attend(0)
    for k in range(1, planes):
        @pl.when(k <= plane)
        def _(k=k):
            for d in range(GROUP):
                from_below(k - 1, d).wait_recv()
                if k < planes - 1:
                    send_up(k, d)
            attend(k)

    def finish(b, dst):
        for h in range(2):
            cols = slice(h * 128, (h + 1) * 128)
            total = jnp.sum(den[b, :, cols], axis=1, keepdims=True)
            dst[b, :, cols] = (acc[b, :, cols] / total).astype(bf16)

    o_copies = {}
    for d in range(1, GROUP):
        b = (place + d) % GROUP
        finish(b, o_send)
        o_copies[d] = copy(o_send.at[b], o_buf.at[place], o_ssem.at[d], o_rsem.at[d], peer(d))
        o_copies[d].start()
    finish(place, o_buf)
    load_wo.wait()
    for d in range(1, GROUP):
        slot = o_buf.at[(place + GROUP - d) % GROUP]
        copy(slot, slot, o_ssem.at[d], o_rsem.at[d], peer(d)).wait_recv()

    part = y_send.shape[2]
    half = tok // 2
    y_copies = []
    for n in range(y_send.shape[0]):
        cols = slice(n * part, (n + 1) * part)
        total = jnp.dot(o_buf[0], wo_v[0:256, cols], preferred_element_type=f32)
        for b in range(1, GROUP):
            total = total + jnp.dot(
                o_buf[b], wo_v[b * 256 : (b + 1) * 256, cols], preferred_element_type=f32
            )
        y_send[n] = jnp.where(core == 0, total[half:], total[:half]).astype(bf16)
        y_copies.append(copy(y_send.at[n], y_recv.at[n], y_ssem.at[n], y_rsem.at[n], mate))
        y_copies[n].start()
        y_mine[n] = jnp.where(core == 0, total[:half], total[half:])
    for n in range(y_send.shape[0]):
        y_copies[n].wait_recv()
        out[:, n * part : (n + 1) * part] = (y_mine[n] + y_recv[n].astype(f32)).astype(bf16)
    for n in range(y_send.shape[0]):
        y_copies[n].wait_send()
    for d in range(1, GROUP):
        kv_copies[d].wait_send()
        q_copies[d].wait_send()
        o_copies[d].wait_send()
    for k in range(planes - 1):
        @pl.when((plane < planes - 1) & (k <= plane))
        def _(k=k):
            for d in range(GROUP):
                up(k, d).wait_send()


def on_device_fused(hidden_in, norm_gain, w_query, w_key, w_value, w_out, q_gain, k_gain, lengths, blocks=16):
    tok, feat = hidden_in.shape
    width = w_out.shape[1]
    f32, bf16 = jnp.float32, jnp.bfloat16
    half_freq = rope_base ** (-np.arange(64, dtype=np.float64) * 2.0 / 128)
    freq = np.concatenate([half_freq, half_freq]).astype(np.float32)[None, :]
    planes = blocks // GROUP
    part = width // 5
    vmem = pl.BlockSpec(memory_space=pltpu.VMEM)
    any_space = pl.BlockSpec(memory_space=pl.ANY)
    dma = pltpu.SemaphoreType.DMA
    return pl.pallas_call(
        fused_kernel,
        out_shape=(
            jax.ShapeDtypeStruct((tok // 2, width), bf16),
            jax.ShapeDtypeStruct((tok, w_key.shape[1]), bf16),
            jax.ShapeDtypeStruct((tok, w_value.shape[1]), bf16),
        ),
        in_specs=[vmem, vmem, any_space, any_space, any_space, any_space, vmem, vmem, vmem,
                  pl.BlockSpec(memory_space=pltpu.SMEM)],
        out_specs=(vmem, vmem, vmem),
        scratch_shapes=[
            pltpu.VMEM((tok, feat), bf16),
            pltpu.VMEM((2, feat, w_query.shape[1]), bf16),
            pltpu.VMEM((2, feat, w_key.shape[1]), bf16),
            pltpu.VMEM((2, feat, w_value.shape[1]), bf16),
            pltpu.VMEM(w_out.shape, bf16),
            pltpu.VMEM((GROUP, tok, 256), bf16),
            pltpu.VMEM((GROUP, tok, 256), bf16),
            pltpu.VMEM((blocks, tok, 256), bf16),
            pltpu.VMEM((GROUP, tok, 256), bf16),
            pltpu.VMEM((GROUP, tok, 256), bf16),
            pltpu.VMEM((GROUP, tok, 256), bf16),
            pltpu.VMEM((GROUP, tok, 128), jnp.int32),
            pltpu.VMEM((GROUP, tok, 256), f32),
            pltpu.VMEM((GROUP, tok, 256), f32),
            pltpu.VMEM((5, tok // 2, part), bf16),
            pltpu.VMEM((5, tok // 2, part), bf16),
            pltpu.VMEM((5, tok // 2, part), f32),
            dma((7,)),
            dma((2,)),
            dma((GROUP,)),
            dma((GROUP,)),
            dma((GROUP,)),
            dma((GROUP,)),
            dma((planes - 1, GROUP)),
            dma((planes - 1, GROUP)),
            dma((GROUP,)),
            dma((GROUP,)),
            dma((5,)),
            dma((5,)),
        ],
        compiler_params=pltpu.CompilerParams(
            collective_id=0, has_side_effects=True, vmem_limit_bytes=44 * 1024 * 1024
        ),
        cost_estimate=pl.CostEstimate(
            flops=3_100_000_000, bytes_accessed=17_000_000, transcendentals=2_200_000
        ),
    )(hidden_in, norm_gain.reshape(2, 1, feat), w_query, w_key, w_value, w_out,
      q_gain.reshape(1, 128), k_gain.reshape(1, 128), freq, lengths)


def solution(mesh):
    seq, tensor = mesh.shape["seq"], mesh.shape["tensor"]
    fits = tensor == 2 and seq % GROUP == 0 and seq <= 16
    body = functools.partial(on_device_fused, blocks=seq) if fits else on_device
    placed = (
        P("seq", "tensor"),
        P(),
        P(None, "tensor"),
        P(None, "tensor"),
        P(None, "tensor"),
        P("tensor", None),
        P(),
        P(),
        P(),
    )
    return jax.shard_map(
        body,
        mesh=mesh,
        in_specs=placed,
        out_specs=(P(("seq", "tensor"), None), P("seq", "tensor"), P("seq", "tensor")),
        check_vma=False,
    )
```

```python
import functools
import math

import jax
import jax.numpy as jnp
import numpy as np
from jax import lax
from jax.experimental import pallas as pl
from jax.experimental.pallas import tpu as pltpu
from jax.sharding import PartitionSpec as P

rope_base = 1000000.0
norm_eps = 1e-06
masked = -1e30


def prompt_starts(lengths, token_pos):
    ends = jnp.cumsum(lengths)
    starts = ends - lengths
    before = (ends[None, :] <= token_pos[:, None]).astype(jnp.int32)
    segment = jnp.sum(before, axis=1)
    onehot = segment[:, None] == jnp.arange(lengths.shape[0], dtype=jnp.int32)[None, :]
    return jnp.sum(jnp.where(onehot, starts[None, :], 0), axis=1)


def head_norm_rope(values, gain, rel_pos):
    width = values.shape[-1]
    half = width // 2
    mean_sq = jnp.mean(values * values, axis=-1, keepdims=True)
    normed = values * lax.rsqrt(mean_sq + norm_eps) * gain
    freq = rope_base ** (-jnp.arange(half, dtype=jnp.float32) * 2.0 / width)
    angle = rel_pos.astype(jnp.float32)[:, None] * freq[None, :]
    cosine = jnp.cos(angle)[:, None, :]
    sine = jnp.sin(angle)[:, None, :]
    first = normed[..., :half]
    second = normed[..., half:]
    return jnp.concatenate(
        [first * cosine - second * sine, second * cosine + first * sine], axis=-1
    )


def on_device(hidden_in, norm_gain, w_query, w_key, w_value, w_out, q_gain, k_gain, lengths):
    tokens = hidden_in.shape[0]
    width = w_query.shape[0]
    head_dim = q_gain.shape[0]
    q_cols = w_query.shape[1]
    kv_cols = w_key.shape[1]
    kv_local = kv_cols // head_dim
    group = q_cols // kv_cols
    combined = jnp.concatenate([w_query, w_key, w_value], axis=1)
    piece = lax.all_gather(hidden_in, "tensor", axis=1, tiled=True)
    wide = piece.astype(jnp.float32)
    rows = combined
    scaled = (wide * norm_gain[None, :]).astype(jnp.bfloat16)
    acc = jnp.dot(scaled, rows, preferred_element_type=jnp.float32)
    acc, sumsq = (acc, jnp.sum(wide * wide, axis=1))
    proj = acc * lax.rsqrt(sumsq / width + norm_eps)[:, None]
    block_index = lax.axis_index("seq")
    token_pos = block_index * tokens + jnp.arange(tokens, dtype=jnp.int32)
    seg_start = prompt_starts(lengths, token_pos)
    rel_pos = token_pos - seg_start
    queries = head_norm_rope(
        proj[:, :q_cols].reshape(tokens, kv_local * group, head_dim), q_gain, rel_pos
    ).astype(jnp.bfloat16)
    keys = head_norm_rope(
        proj[:, q_cols : q_cols + kv_cols].reshape(tokens, kv_local, head_dim), k_gain, rel_pos
    ).astype(jnp.bfloat16)
    key_flat = keys.reshape(tokens, kv_cols)
    value_flat = proj[:, q_cols + kv_cols :].astype(jnp.bfloat16)
    query_grid = queries.reshape(tokens, kv_local, group, head_dim)
    inv_root = 1.0 / math.sqrt(head_dim)
    last_pos = jnp.max(token_pos)
    first_start = jnp.min(seg_start)

    def attend_block(carry, key_block, value_block, key_start):
        rows = key_block.shape[0]
        key_pos = key_start + jnp.arange(rows, dtype=jnp.int32)

        def compute(state):
            best, total, summed = state
            key_heads = key_block.reshape(rows, kv_local, head_dim)
            value_heads = value_block.reshape(rows, kv_local, head_dim)
            score = (
                jnp.einsum(
                    "qhgd,khd->hgqk", query_grid, key_heads, preferred_element_type=jnp.float32
                )
                * inv_root
            )
            visible = (key_pos[None, :] >= seg_start[:, None]) & (
                key_pos[None, :] <= token_pos[:, None]
            )
            score = jnp.where(visible[None, None], score, masked)
            fresh = jnp.maximum(best, jnp.max(score, axis=-1))
            weights = jnp.where(visible[None, None], jnp.exp(score - fresh[..., None]), 0.0)
            decay = jnp.exp(best - fresh)
            total = total * decay + jnp.sum(weights, axis=-1)
            summed = summed * decay[..., None] + jnp.einsum(
                "hgqk,khd->hgqd",
                weights.astype(jnp.bfloat16),
                value_heads,
                preferred_element_type=jnp.float32,
            )
            return (fresh, total, summed)

        seen = (key_start <= last_pos) & (key_start + rows - 1 >= first_start)
        return lax.cond(seen, compute, lambda state: state, carry)

    start_state = (
        jnp.full((kv_local, group, tokens), masked, jnp.float32),
        jnp.zeros((kv_local, group, tokens), jnp.float32),
        jnp.zeros((kv_local, group, tokens, head_dim), jnp.float32),
    )
    key_piece = lax.all_gather(key_flat, "seq", axis=0, tiled=True)
    value_piece = lax.all_gather(value_flat, "seq", axis=0, tiled=True)
    rows = key_piece.shape[0]
    size = math.gcd(rows, 512)
    count = rows // size

    def one_part(state, part):
        key_part, value_part, offset = part
        return (attend_block(state, key_part, value_part, offset), None)

    offsets = jnp.arange(count, dtype=jnp.int32) * size
    parts = (
        key_piece.reshape(count, size, kv_cols),
        value_piece.reshape(count, size, kv_cols),
        offsets,
    )
    state, unused = lax.scan(one_part, start_state, parts)
    best, total, summed = state
    attn = summed / total[..., None]
    attn = jnp.transpose(attn, (2, 0, 1, 3)).reshape(tokens, q_cols).astype(jnp.bfloat16)
    mixed = lax.psum_scatter(
        jnp.dot(attn, w_out, preferred_element_type=jnp.float32).astype(jnp.bfloat16),
        "tensor",
        scatter_dimension=0,
        tiled=True,
    )
    return (mixed, key_flat, value_flat)


GROUP = 4


def fused_kernel(
    hid_in, gain_in, wq, wk, wv, wo, q_gain_in, k_gain_in, freq_in, lens_in,
    out_hbm, key_hbm, value_hbm,
    out, key_out, value_out, hid, gain, q_gain, k_gain, freq, lens,
    peer_hid, wq_v, wkv_v, wo_v, kv_send, q_send, kv_buf, q_buf, o_send, o_buf,
    seg_q, acc, den, kv_acc, q_acc, y_send, y_recv, y_mine,
    in_sem, wkv_sem, wq_sem, wo_sem, h_sem, kv_ssem, kv_rsem, q_ssem, q_rsem,
    z_ssem, z_rsem, o_ssem, o_rsem, y_ssem, y_rsem, out_sem,
):
    f32, bf16 = jnp.float32, jnp.bfloat16
    tok, feat = hid.shape
    seq = lax.axis_index("seq")
    core = lax.axis_index("tensor")
    planes = kv_buf.shape[0] // GROUP
    plane = seq // GROUP
    place = seq % GROUP
    mate = (seq, 1 - core)
    above = (seq + GROUP, core)
    below = (seq - GROUP, core)

    def peer(d):
        return (plane * GROUP + (place + d) % GROUP, core)

    def copy(src, dst, ssem, rsem, device):
        return pltpu.make_async_remote_copy(
            src_ref=src, dst_ref=dst, send_sem=ssem, recv_sem=rsem,
            device_id=device, device_id_type=pl.DeviceIdType.MESH,
        )

    barrier = pltpu.get_barrier_semaphore()

    def greet(device):
        pl.semaphore_signal(barrier, inc=1, device_id=device, device_id_type=pl.DeviceIdType.MESH)

    greet(mate)
    for d in range(1, GROUP):
        greet(peer(d))

    @pl.when(plane < planes - 1)
    def _():
        greet(above)

    @pl.when(plane > 0)
    def _():
        greet(below)

    halves = (core, 1 - core)
    small = []
    for src, dst in (
        (hid_in, hid),
        (lens_in, lens),
        (freq_in, freq),
        (gain_in.at[:, pl.ds(pl.multiple_of(halves[0] * feat, 128), feat)], gain.at[0]),
        (gain_in.at[:, pl.ds(pl.multiple_of(halves[1] * feat, 128), feat)], gain.at[1]),
        (q_gain_in, q_gain),
        (k_gain_in, k_gain),
    ):
        small.append(pltpu.make_async_copy(src, dst, in_sem.at[len(small)]))
        small[-1].start()

    def rows(i):
        return pl.ds(pl.multiple_of(halves[i] * feat, feat), feat)

    kv_loads, q_loads = {}, {}
    for i in range(2):
        for d in range(GROUP):
            cols = pl.ds(pl.multiple_of((place + d) % GROUP * 128, 128), 128)
            for n, w in enumerate((wk, wv)):
                kv_loads[i, d, n] = pltpu.make_async_copy(
                    w.at[rows(i), cols], wkv_v.at[i, d, :, n * 128 : (n + 1) * 128], wkv_sem.at[i, d, n]
                )
                kv_loads[i, d, n].start()
    for i in range(2):
        q_loads[i] = pltpu.make_async_copy(wq.at[rows(i)], wq_v.at[i], wq_sem.at[i])
        q_loads[i].start()
    load_wo = pltpu.make_async_copy(wo, wo_v, wo_sem)
    load_wo.start()

    for load in small:
        load.wait()

    lengths = [lens[j] for j in range(lens.shape[0])]
    ends, run = [], jnp.int32(0)
    for length in lengths:
        run = run + length
        ends.append(run)
    for b in range(GROUP):
        pos = lax.broadcasted_iota(jnp.int32, (tok, 128), 0) + (plane * GROUP + b) * tok
        start = jnp.zeros((tok, 128), jnp.int32)
        for length, end in zip(lengths, ends):
            start = start + jnp.where(end <= pos, length, 0)
        seg_q[b] = start
    own_pos = lax.broadcasted_iota(jnp.int32, (tok, 128), 0) + seq * tok
    angle = (own_pos - seg_q[place]).astype(f32) * freq[...]
    cosine = jnp.cos(angle)
    lane = lax.broadcasted_iota(jnp.int32, (tok, 128), 1)
    sine = jnp.where(lane < 64, -jnp.sin(angle), jnp.sin(angle))

    x_own = hid[...].astype(f32)
    scaled_own = (x_own * gain[0]).astype(bf16)
    sum_own = jnp.sum(x_own * x_own, axis=1, keepdims=True)
    for d in range(GROUP):
        for n in range(2):
            kv_loads[0, d, n].wait()
        kv_acc[d] = jnp.dot(scaled_own, wkv_v[0, d], preferred_element_type=f32)

    neighbours = (plane + planes - 1) // planes + (2 * planes - 2 - plane) // planes
    pl.semaphore_wait(barrier, GROUP + neighbours)
    hid_copy = copy(hid, peer_hid, h_sem.at[0], h_sem.at[1], mate)
    hid_copy.start()

    def q_cols(d):
        return pl.ds(pl.multiple_of((place + d) % GROUP * 256, 256), 256)

    q_loads[0].wait()
    for d in range(GROUP):
        q_acc[d] = jnp.dot(scaled_own, wq_v[0, :, q_cols(d)], preferred_element_type=f32)

    hid_copy.wait()
    x_far = peer_hid[...].astype(f32)
    scaled_far = (x_far * gain[1]).astype(bf16)
    sumsq = sum_own + jnp.sum(x_far * x_far, axis=1, keepdims=True)
    inv = lax.rsqrt(sumsq / (2 * feat) + norm_eps)

    def rope(u, g):
        u = u * lax.rsqrt(jnp.mean(u * u, axis=1, keepdims=True) + norm_eps) * g[...]
        return (u * cosine + pltpu.roll(u, 64, 1) * sine).astype(bf16)

    def up(k, d):
        slot = kv_buf.at[(plane - k) * GROUP + (place + GROUP - d) % GROUP]
        return copy(slot, slot, z_ssem.at[k, d], z_rsem.at[k, d], above)

    def from_below(k, d):
        slot = kv_buf.at[(plane - 1 - k) * GROUP + (place + GROUP - d) % GROUP]
        return copy(slot, slot, z_ssem.at[k, d], z_rsem.at[k, d], below)

    def send_up(k, d):
        @pl.when(plane < planes - 1)
        def _():
            up(k, d).start()

    kv_copies, q_copies = {}, {}
    for d in range(GROUP):
        for n in range(2):
            kv_loads[1, d, n].wait()
        pair = kv_acc[d] + jnp.dot(scaled_far, wkv_v[1, d], preferred_element_type=f32)
        pair = pair * inv
        key = rope(pair[:, :128], k_gain)
        value = pair[:, 128:].astype(bf16)
        cols = pl.ds(pl.multiple_of((place + d) % GROUP * 128, 128), 128)
        key_out[:, cols] = key
        value_out[:, cols] = value
        if d == 0:
            kv_buf[seq, :, :128] = key
            kv_buf[seq, :, 128:] = value
            send_up(0, 0)
        else:
            kv_send[d, :, :128] = key
            kv_send[d, :, 128:] = value
            kv_copies[d] = copy(kv_send.at[d], kv_buf.at[seq], kv_ssem.at[d], kv_rsem.at[d], peer(d))
            kv_copies[d].start()

    stores = [
        pltpu.make_async_copy(src, dst, out_sem.at[n])
        for n, (src, dst) in enumerate(((key_out, key_hbm), (value_out, value_hbm), (out, out_hbm)))
    ]
    stores[0].start()
    stores[1].start()

    def kv_arrival(d):
        slot = kv_buf.at[plane * GROUP + (place + GROUP - d) % GROUP]
        return copy(slot, slot, kv_ssem.at[d], kv_rsem.at[d], peer(d))

    q_loads[1].wait()
    for turn, d in enumerate((1, 2, 3, 0)):
        pair = q_acc[d] + jnp.dot(scaled_far, wq_v[1, :, q_cols(d)], preferred_element_type=f32)
        pair = pair * inv
        for i in range(2):
            query = rope(pair[:, i * 128 : (i + 1) * 128], q_gain)
            if d == 0:
                q_buf[place, i * tok : (i + 1) * tok] = query
            else:
                q_send[d, i * tok : (i + 1) * tok] = query
        if d > 0:
            q_copies[d] = copy(q_send.at[d], q_buf.at[place], q_ssem.at[d], q_rsem.at[d], peer(d))
            q_copies[d].start()
        if turn >= 1:
            kv_arrival(turn).wait_recv()
            send_up(0, turn)

    @pl.when(plane >= 1)
    def _():
        for d in range(GROUP):
            from_below(0, d).wait_recv()
            send_up(1, d)

    for d in range(1, GROUP):
        slot = q_buf.at[(place + GROUP - d) % GROUP]
        copy(slot, slot, q_ssem.at[d], q_rsem.at[d], peer(d)).wait_recv()

    scale = math.log2(math.e) / math.sqrt(128)

    def o_copy(i):
        b = (place + 1 + i) % GROUP
        return copy(o_send.at[b], o_buf.at[place], o_ssem.at[i], o_rsem.at[i], (plane * GROUP + b, core))

    def attend(k, pieces, ends_plane):
        slots = [(plane - k) * GROUP + (place + GROUP - d) % GROUP for d in pieces]
        span = 128 * len(pieces)
        lanes = lax.broadcasted_iota(jnp.int32, (tok, 128), 1)
        key_pos = jnp.concatenate([lanes + slot * tok for slot in slots], axis=1)
        fresh = k == 0 and pieces[0] == 0

        def one_block(i, carry):
            b = (place + 1 + i) % GROUP
            keys = jnp.concatenate([kv_buf[slot, :, :128] for slot in slots], axis=0)
            values = jnp.concatenate([kv_buf[slot, :, 128:] for slot in slots], axis=0)
            start = jnp.concatenate([seg_q[b]] * len(pieces), axis=1)
            visible = key_pos >= start
            if k == 0:
                q_pos = lax.broadcasted_iota(jnp.int32, (tok, span), 0) + (plane * GROUP + b) * tok
                visible = visible & (key_pos <= q_pos)
            score = lax.dot_general(
                q_buf[b], keys, (((1,), (1,)), ((), ())), preferred_element_type=f32
            )
            rounded = []
            for h in range(2):
                weights = jnp.where(visible, jnp.exp2(score[h * tok : (h + 1) * tok] * scale), 0.0)
                part = weights[:, :128]
                for n in range(1, len(pieces)):
                    part = part + weights[:, n * 128 : (n + 1) * 128]
                if fresh:
                    den[b, h * tok : (h + 1) * tok] = part
                else:
                    den[b, h * tok : (h + 1) * tok] += part
                rounded.append(weights.astype(bf16))
            summed = jnp.dot(jnp.concatenate(rounded, axis=0), values, preferred_element_type=f32)
            if fresh:
                acc[b] = summed
            else:
                acc[b] += summed
            if ends_plane:
                @pl.when(plane == k)
                def _():
                    for h in range(2):
                        part = slice(h * tok, (h + 1) * tok)
                        total = jnp.sum(den[b, part], axis=1, keepdims=True)
                        o_send[b, :, h * 128 : (h + 1) * 128] = (acc[b, part] / total).astype(bf16)

                    @pl.when(i < GROUP - 1)
                    def _():
                        o_copy(i).start()

            return carry

        lax.fori_loop(0, GROUP, one_block, 0)

    attend(0, (0, 1, 2, 3), True)
    for k in range(1, planes):
        @pl.when(k <= plane)
        def _(k=k):
            if k < planes - 1:
                if k > 1:
                    for d in range(GROUP):
                        from_below(k - 1, d).wait_recv()
                        send_up(k, d)
                attend(k, (0, 1, 2, 3), True)
            else:
                for pieces in ((0, 1, 2), (3,)):
                    for d in pieces:
                        if k > 1:
                            from_below(k - 1, d).wait_recv()
                    attend(k, pieces, pieces[-1] == GROUP - 1)

    o_buf[place] = o_send[place]
    load_wo.wait()
    for i in range(GROUP - 1):
        slot = o_buf.at[(place + 2 * GROUP - 1 - i) % GROUP]
        copy(slot, slot, o_ssem.at[i], o_rsem.at[i], peer(i + 1)).wait_recv()

    part = y_send.shape[2]
    half = tok // 2
    y_copies = []
    for n in range(y_send.shape[0]):
        cols = slice(n * part, (n + 1) * part)
        total = jnp.dot(o_buf[0], wo_v[0:256, cols], preferred_element_type=f32)
        for b in range(1, GROUP):
            total = total + jnp.dot(
                o_buf[b], wo_v[b * 256 : (b + 1) * 256, cols], preferred_element_type=f32
            )
        y_send[n] = jnp.where(core == 0, total[half:], total[:half]).astype(bf16)
        y_copies.append(copy(y_send.at[n], y_recv.at[n], y_ssem.at[n], y_rsem.at[n], mate))
        y_copies[n].start()
        y_mine[n] = jnp.where(core == 0, total[:half], total[half:])
    for n in range(y_send.shape[0]):
        y_copies[n].wait_recv()
        out[:, n * part : (n + 1) * part] = (y_mine[n] + y_recv[n].astype(f32)).astype(bf16)
    stores[2].start()
    for n in range(y_send.shape[0]):
        y_copies[n].wait_send()
    for d in range(1, GROUP):
        kv_copies[d].wait_send()
        q_copies[d].wait_send()
        o_copy(d - 1).wait_send()
    for k in range(planes - 1):
        @pl.when((plane < planes - 1) & (k <= plane))
        def _(k=k):
            for d in range(GROUP):
                up(k, d).wait_send()
    for store in stores:
        store.wait()


def store_kernel(a, b, c, a_out, b_out, c_out, sem):
    stores = [
        pltpu.make_async_copy(src, dst, sem.at[n])
        for n, (src, dst) in enumerate(((a, a_out), (b, b_out), (c, c_out)))
    ]
    for store in stores:
        store.start()
    for store in stores:
        store.wait()


def on_device_fused(hidden_in, norm_gain, w_query, w_key, w_value, w_out, q_gain, k_gain, lengths, blocks=16):
    tok, feat = hidden_in.shape
    width = w_out.shape[1]
    f32, bf16 = jnp.float32, jnp.bfloat16
    half_freq = rope_base ** (-np.arange(64, dtype=np.float64) * 2.0 / 128)
    freq = np.concatenate([half_freq, half_freq]).astype(np.float32)[None, :]
    planes = blocks // GROUP
    part = width // 5
    hbm = pl.BlockSpec(memory_space=pltpu.HBM)
    dma = pltpu.SemaphoreType.DMA
    shapes = (
        jax.ShapeDtypeStruct((tok // 2, width), bf16),
        jax.ShapeDtypeStruct((tok, w_key.shape[1]), bf16),
        jax.ShapeDtypeStruct((tok, w_value.shape[1]), bf16),
    )
    results = pl.pallas_call(
        fused_kernel,
        out_shape=shapes,
        in_specs=[hbm] * 10,
        out_specs=(hbm, hbm, hbm),
        scratch_shapes=[
            *[pltpu.VMEM(shape.shape, bf16) for shape in shapes],
            pltpu.VMEM((tok, feat), bf16),
            pltpu.VMEM((2, 1, feat), f32),
            pltpu.VMEM((1, 128), f32),
            pltpu.VMEM((1, 128), f32),
            pltpu.VMEM((1, 128), f32),
            pltpu.SMEM(lengths.shape, jnp.int32),
            pltpu.VMEM((tok, feat), bf16),
            pltpu.VMEM((2, feat, w_query.shape[1]), bf16),
            pltpu.VMEM((2, GROUP, feat, 256), bf16),
            pltpu.VMEM(w_out.shape, bf16),
            pltpu.VMEM((GROUP, tok, 256), bf16),
            pltpu.VMEM((GROUP, 2 * tok, 128), bf16),
            pltpu.VMEM((blocks, tok, 256), bf16),
            pltpu.VMEM((GROUP, 2 * tok, 128), bf16),
            pltpu.VMEM((GROUP, tok, 256), bf16),
            pltpu.VMEM((GROUP, tok, 256), bf16),
            pltpu.VMEM((GROUP, tok, 128), jnp.int32),
            pltpu.VMEM((GROUP, 2 * tok, 128), f32),
            pltpu.VMEM((GROUP, 2 * tok, 128), f32),
            pltpu.VMEM((GROUP, tok, 256), f32),
            pltpu.VMEM((GROUP, tok, 256), f32),
            pltpu.VMEM((5, tok // 2, part), bf16),
            pltpu.VMEM((5, tok // 2, part), bf16),
            pltpu.VMEM((5, tok // 2, part), f32),
            dma((7,)),
            dma((2, GROUP, 2)),
            dma((2,)),
            dma,
            dma((2,)),
            dma((GROUP,)),
            dma((GROUP,)),
            dma((GROUP,)),
            dma((GROUP,)),
            dma((planes - 1, GROUP)),
            dma((planes - 1, GROUP)),
            dma((GROUP,)),
            dma((GROUP,)),
            dma((5,)),
            dma((5,)),
            dma((3,)),
        ],
        compiler_params=pltpu.CompilerParams(
            collective_id=0, has_side_effects=True, vmem_limit_bytes=63 * 1024 * 1024
        ),
        cost_estimate=pl.CostEstimate(
            flops=3_100_000_000, bytes_accessed=17_000_000, transcendentals=2_200_000
        ),
    )(hidden_in, norm_gain.reshape(1, 2 * feat), w_query, w_key, w_value, w_out,
      q_gain.reshape(1, 128), k_gain.reshape(1, 128), freq, lengths)
    return pl.pallas_call(
        store_kernel,
        out_shape=shapes,
        in_specs=[pl.BlockSpec(memory_space=pl.ANY)] * 3,
        out_specs=(hbm, hbm, hbm),
        scratch_shapes=[dma((3,))],
        compiler_params=pltpu.CompilerParams(vmem_limit_bytes=63 * 1024 * 1024),
    )(*results)


def solution(mesh):
    seq, tensor = mesh.shape["seq"], mesh.shape["tensor"]
    fits = tensor == 2 and seq % GROUP == 0 and seq <= 16
    body = functools.partial(on_device_fused, blocks=seq) if fits else on_device
    placed = (
        P("seq", "tensor"),
        P(),
        P(None, "tensor"),
        P(None, "tensor"),
        P(None, "tensor"),
        P("tensor", None),
        P(),
        P(),
        P(),
    )
    return jax.shard_map(
        body,
        mesh=mesh,
        in_specs=placed,
        out_specs=(P(("seq", "tensor"), None), P("seq", "tensor"), P("seq", "tensor")),
        check_vma=False,
    )
```

```python
import functools
import math

import jax
import jax.numpy as jnp
import numpy as np
from jax import lax
from jax.experimental import pallas as pl
from jax.experimental.pallas import tpu as pltpu
from jax.sharding import PartitionSpec as P

rope_base = 1000000.0
norm_eps = 1e-06
masked = -1e30


def prompt_starts(lengths, token_pos):
    ends = jnp.cumsum(lengths)
    starts = ends - lengths
    before = (ends[None, :] <= token_pos[:, None]).astype(jnp.int32)
    segment = jnp.sum(before, axis=1)
    onehot = segment[:, None] == jnp.arange(lengths.shape[0], dtype=jnp.int32)[None, :]
    return jnp.sum(jnp.where(onehot, starts[None, :], 0), axis=1)


def head_norm_rope(values, gain, rel_pos):
    width = values.shape[-1]
    half = width // 2
    mean_sq = jnp.mean(values * values, axis=-1, keepdims=True)
    normed = values * lax.rsqrt(mean_sq + norm_eps) * gain
    freq = rope_base ** (-jnp.arange(half, dtype=jnp.float32) * 2.0 / width)
    angle = rel_pos.astype(jnp.float32)[:, None] * freq[None, :]
    cosine = jnp.cos(angle)[:, None, :]
    sine = jnp.sin(angle)[:, None, :]
    first = normed[..., :half]
    second = normed[..., half:]
    return jnp.concatenate(
        [first * cosine - second * sine, second * cosine + first * sine], axis=-1
    )


def on_device(hidden_in, norm_gain, w_query, w_key, w_value, w_out, q_gain, k_gain, lengths):
    tokens = hidden_in.shape[0]
    width = w_query.shape[0]
    head_dim = q_gain.shape[0]
    q_cols = w_query.shape[1]
    kv_cols = w_key.shape[1]
    kv_local = kv_cols // head_dim
    group = q_cols // kv_cols
    combined = jnp.concatenate([w_query, w_key, w_value], axis=1)
    piece = lax.all_gather(hidden_in, "tensor", axis=1, tiled=True)
    wide = piece.astype(jnp.float32)
    rows = combined
    scaled = (wide * norm_gain[None, :]).astype(jnp.bfloat16)
    acc = jnp.dot(scaled, rows, preferred_element_type=jnp.float32)
    acc, sumsq = (acc, jnp.sum(wide * wide, axis=1))
    proj = acc * lax.rsqrt(sumsq / width + norm_eps)[:, None]
    block_index = lax.axis_index("seq")
    token_pos = block_index * tokens + jnp.arange(tokens, dtype=jnp.int32)
    seg_start = prompt_starts(lengths, token_pos)
    rel_pos = token_pos - seg_start
    queries = head_norm_rope(
        proj[:, :q_cols].reshape(tokens, kv_local * group, head_dim), q_gain, rel_pos
    ).astype(jnp.bfloat16)
    keys = head_norm_rope(
        proj[:, q_cols : q_cols + kv_cols].reshape(tokens, kv_local, head_dim), k_gain, rel_pos
    ).astype(jnp.bfloat16)
    key_flat = keys.reshape(tokens, kv_cols)
    value_flat = proj[:, q_cols + kv_cols :].astype(jnp.bfloat16)
    query_grid = queries.reshape(tokens, kv_local, group, head_dim)
    inv_root = 1.0 / math.sqrt(head_dim)
    last_pos = jnp.max(token_pos)
    first_start = jnp.min(seg_start)

    def attend_block(carry, key_block, value_block, key_start):
        rows = key_block.shape[0]
        key_pos = key_start + jnp.arange(rows, dtype=jnp.int32)

        def compute(state):
            best, total, summed = state
            key_heads = key_block.reshape(rows, kv_local, head_dim)
            value_heads = value_block.reshape(rows, kv_local, head_dim)
            score = (
                jnp.einsum(
                    "qhgd,khd->hgqk", query_grid, key_heads, preferred_element_type=jnp.float32
                )
                * inv_root
            )
            visible = (key_pos[None, :] >= seg_start[:, None]) & (
                key_pos[None, :] <= token_pos[:, None]
            )
            score = jnp.where(visible[None, None], score, masked)
            fresh = jnp.maximum(best, jnp.max(score, axis=-1))
            weights = jnp.where(visible[None, None], jnp.exp(score - fresh[..., None]), 0.0)
            decay = jnp.exp(best - fresh)
            total = total * decay + jnp.sum(weights, axis=-1)
            summed = summed * decay[..., None] + jnp.einsum(
                "hgqk,khd->hgqd",
                weights.astype(jnp.bfloat16),
                value_heads,
                preferred_element_type=jnp.float32,
            )
            return (fresh, total, summed)

        seen = (key_start <= last_pos) & (key_start + rows - 1 >= first_start)
        return lax.cond(seen, compute, lambda state: state, carry)

    start_state = (
        jnp.full((kv_local, group, tokens), masked, jnp.float32),
        jnp.zeros((kv_local, group, tokens), jnp.float32),
        jnp.zeros((kv_local, group, tokens, head_dim), jnp.float32),
    )
    key_piece = lax.all_gather(key_flat, "seq", axis=0, tiled=True)
    value_piece = lax.all_gather(value_flat, "seq", axis=0, tiled=True)
    rows = key_piece.shape[0]
    size = math.gcd(rows, 512)
    count = rows // size

    def one_part(state, part):
        key_part, value_part, offset = part
        return (attend_block(state, key_part, value_part, offset), None)

    offsets = jnp.arange(count, dtype=jnp.int32) * size
    parts = (
        key_piece.reshape(count, size, kv_cols),
        value_piece.reshape(count, size, kv_cols),
        offsets,
    )
    state, unused = lax.scan(one_part, start_state, parts)
    best, total, summed = state
    attn = summed / total[..., None]
    attn = jnp.transpose(attn, (2, 0, 1, 3)).reshape(tokens, q_cols).astype(jnp.bfloat16)
    mixed = lax.psum_scatter(
        jnp.dot(attn, w_out, preferred_element_type=jnp.float32).astype(jnp.bfloat16),
        "tensor",
        scatter_dimension=0,
        tiled=True,
    )
    return (mixed, key_flat, value_flat)


GROUP = 4


def fused_kernel(
    hid_in, gain_in, wq, wk, wv, wo, q_gain_in, k_gain_in, freq_in, lens_in,
    out_hbm, key_hbm, value_hbm,
    out, key_out, value_out, hid, gain, q_gain, k_gain, freq, lens,
    peer_hid, wq_v, wkv_v, wo_v, kv_send, q_send, kv_buf, q_buf, o_send, o_buf,
    seg_q, acc, den, kv_acc, y_acc, y_send, y_recv, y_mine,
    in_sem, wkv_sem, wq_sem, wo_sem, h_sem, kv_ssem, kv_rsem, q_ssem, q_rsem,
    z_ssem, z_rsem, o_ssem, o_rsem, y_ssem, y_rsem, out_sem,
):
    f32, bf16 = jnp.float32, jnp.bfloat16
    tok, feat = hid.shape
    seq = lax.axis_index("seq")
    core = lax.axis_index("tensor")
    planes = kv_buf.shape[0] // GROUP
    plane = seq // GROUP
    place = seq % GROUP
    mate = (seq, 1 - core)
    above = (seq + GROUP, core)
    below = (seq - GROUP, core)

    def peer(d):
        return (plane * GROUP + (place + d) % GROUP, core)

    def copy(src, dst, ssem, rsem, device):
        return pltpu.make_async_remote_copy(
            src_ref=src, dst_ref=dst, send_sem=ssem, recv_sem=rsem,
            device_id=device, device_id_type=pl.DeviceIdType.MESH,
        )

    barrier = pltpu.get_barrier_semaphore()

    def greet(device):
        pl.semaphore_signal(barrier, inc=1, device_id=device, device_id_type=pl.DeviceIdType.MESH)

    greet(mate)
    for d in range(1, GROUP):
        greet(peer(d))

    @pl.when(plane < planes - 1)
    def _():
        greet(above)

    @pl.when(plane > 0)
    def _():
        greet(below)

    halves = (core, 1 - core)
    small = []
    for src, dst in (
        (hid_in, hid),
        (lens_in, lens),
        (freq_in, freq),
        (gain_in, gain),
        (q_gain_in, q_gain),
        (k_gain_in, k_gain),
    ):
        small.append(pltpu.make_async_copy(src, dst, in_sem.at[len(small)]))
        small[-1].start()

    def rows(i):
        return pl.ds(pl.multiple_of(halves[i] * feat, feat), feat)

    kv_loads, q_loads = {}, {}
    for i in range(2):
        for d in range(GROUP):
            cols = pl.ds(pl.multiple_of((place + d) % GROUP * 128, 128), 128)
            for n, w in enumerate((wk, wv)):
                kv_loads[i, d, n] = pltpu.make_async_copy(
                    w.at[rows(i), cols], wkv_v.at[i, d, :, n * 128 : (n + 1) * 128], wkv_sem.at[i, d, n]
                )
                kv_loads[i, d, n].start()
    for i in range(2):
        q_loads[i] = pltpu.make_async_copy(wq.at[rows(i)], wq_v.at[i], wq_sem.at[i])
        q_loads[i].start()
    load_wo = pltpu.make_async_copy(wo, wo_v, wo_sem)
    load_wo.start()

    for load in small:
        load.wait()

    lengths = [lens[j] for j in range(lens.shape[0])]
    ends, run = [], jnp.int32(0)
    for length in lengths:
        run = run + length
        ends.append(run)
    for b in range(GROUP):
        pos = lax.broadcasted_iota(jnp.int32, (tok, 128), 0) + (plane * GROUP + b) * tok
        start = jnp.zeros((tok, 128), jnp.int32)
        for length, end in zip(lengths, ends):
            start = start + jnp.where(end <= pos, length, 0)
        seg_q[b] = start
    own_pos = lax.broadcasted_iota(jnp.int32, (tok, 128), 0) + seq * tok
    angle = (own_pos - seg_q[place]).astype(f32) * freq[...]
    cosine = jnp.cos(angle)
    lane = lax.broadcasted_iota(jnp.int32, (tok, 128), 1)
    sine = jnp.where(lane < 64, -jnp.sin(angle), jnp.sin(angle))

    neighbours = (plane + planes - 1) // planes + (2 * planes - 2 - plane) // planes
    pl.semaphore_wait(barrier, GROUP + neighbours)
    hid_copy = copy(hid, peer_hid, h_sem.at[0], h_sem.at[1], mate)
    hid_copy.start()

    def gain_row(half):
        first = half * (feat // 128)
        return jnp.concatenate([gain[pl.ds(first + r, 1)] for r in range(feat // 128)], axis=1)

    x_own = hid[...].astype(f32)
    scaled_own = (x_own * gain_row(halves[0])).astype(bf16)
    sum_own = jnp.sum(x_own * x_own, axis=1, keepdims=True)
    for d in range(GROUP):
        for n in range(2):
            kv_loads[0, d, n].wait()
        kv_acc[d] = jnp.dot(scaled_own, wkv_v[0, d], preferred_element_type=f32)

    def q_cols(d):
        return pl.ds(pl.multiple_of((place + d) % GROUP * 256, 256), 256)

    hid_copy.wait()
    x_far = peer_hid[...].astype(f32)
    scaled_far = (x_far * gain_row(halves[1])).astype(bf16)
    sumsq = sum_own + jnp.sum(x_far * x_far, axis=1, keepdims=True)
    inv = lax.rsqrt(sumsq / (2 * feat) + norm_eps)

    def rope(u, g):
        u = u * lax.rsqrt(jnp.mean(u * u, axis=1, keepdims=True) + norm_eps) * g[...]
        return (u * cosine + pltpu.roll(u, 64, 1) * sine).astype(bf16)

    def up(k, d):
        slot = kv_buf.at[(plane - k) * GROUP + (place + GROUP - d) % GROUP]
        return copy(slot, slot, z_ssem.at[k, d], z_rsem.at[k, d], above)

    def from_below(k, d):
        slot = kv_buf.at[(plane - 1 - k) * GROUP + (place + GROUP - d) % GROUP]
        return copy(slot, slot, z_ssem.at[k, d], z_rsem.at[k, d], below)

    def send_up(k, d):
        @pl.when(plane < planes - 1)
        def _():
            up(k, d).start()

    kv_copies, q_copies = {}, {}
    for d in range(GROUP):
        for n in range(2):
            kv_loads[1, d, n].wait()
        pair = kv_acc[d] + jnp.dot(scaled_far, wkv_v[1, d], preferred_element_type=f32)
        pair = pair * inv
        key = rope(pair[:, :128], k_gain)
        value = pair[:, 128:].astype(bf16)
        cols = pl.ds(pl.multiple_of((place + d) % GROUP * 128, 128), 128)
        key_out[:, cols] = key
        value_out[:, cols] = value
        if d == 0:
            kv_buf[seq, :, :128] = key
            kv_buf[seq, :, 128:] = value
            send_up(0, 0)
        else:
            kv_send[d, :, :128] = key
            kv_send[d, :, 128:] = value
            kv_copies[d] = copy(kv_send.at[d], kv_buf.at[seq], kv_ssem.at[d], kv_rsem.at[d], peer(d))
            kv_copies[d].start()

    stores = [
        pltpu.make_async_copy(src, dst, out_sem.at[n])
        for n, (src, dst) in enumerate(((key_out, key_hbm), (value_out, value_hbm), (out, out_hbm)))
    ]
    stores[0].start()
    stores[1].start()

    def kv_arrival(d):
        slot = kv_buf.at[plane * GROUP + (place + GROUP - d) % GROUP]
        return copy(slot, slot, kv_ssem.at[d], kv_rsem.at[d], peer(d))

    q_loads[0].wait()
    q_loads[1].wait()
    for turn, d in enumerate((1, 2, 3, 0)):
        pair = jnp.dot(scaled_own, wq_v[0, :, q_cols(d)], preferred_element_type=f32)
        pair = pair + jnp.dot(scaled_far, wq_v[1, :, q_cols(d)], preferred_element_type=f32)
        pair = pair * inv
        for i in range(2):
            query = rope(pair[:, i * 128 : (i + 1) * 128], q_gain)
            if d == 0:
                q_buf[place, i * tok : (i + 1) * tok] = query
            else:
                q_send[d, i * tok : (i + 1) * tok] = query
        if d > 0:
            q_copies[d] = copy(q_send.at[d], q_buf.at[place], q_ssem.at[d], q_rsem.at[d], peer(d))
            q_copies[d].start()
        if turn >= 1:
            kv_arrival(turn).wait_recv()
            send_up(0, turn)

    @pl.when(plane >= 1)
    def _():
        for d in range(GROUP):
            from_below(0, d).wait_recv()
            send_up(1, d)

    for d in range(1, GROUP):
        slot = q_buf.at[(place + GROUP - d) % GROUP]
        copy(slot, slot, q_ssem.at[d], q_rsem.at[d], peer(d)).wait_recv()

    scale = math.log2(math.e) / math.sqrt(128)

    def o_copy(i):
        b = (place + 1 + i) % GROUP
        return copy(o_send.at[b], o_buf.at[place], o_ssem.at[i], o_rsem.at[i], (plane * GROUP + b, core))

    def attend(k, pieces, ends_plane):
        slots = [(plane - k) * GROUP + (place + GROUP - d) % GROUP for d in pieces]
        span = 128 * len(pieces)
        lanes = lax.broadcasted_iota(jnp.int32, (tok, 128), 1)
        key_pos = jnp.concatenate([lanes + slot * tok for slot in slots], axis=1)
        fresh = k == 0 and pieces[0] == 0

        def one_block(i, carry):
            b = (place + 1 + i) % GROUP
            keys = jnp.concatenate([kv_buf[slot, :, :128] for slot in slots], axis=0)
            values = jnp.concatenate([kv_buf[slot, :, 128:] for slot in slots], axis=0)
            start = jnp.concatenate([seg_q[b]] * len(pieces), axis=1)
            visible = key_pos >= start
            if k == 0:
                q_pos = lax.broadcasted_iota(jnp.int32, (tok, span), 0) + (plane * GROUP + b) * tok
                visible = visible & (key_pos <= q_pos)
            score = lax.dot_general(
                q_buf[b], keys, (((1,), (1,)), ((), ())), preferred_element_type=f32
            )
            rounded = []
            for h in range(2):
                weights = jnp.where(visible, jnp.exp2(score[h * tok : (h + 1) * tok] * scale), 0.0)
                part = weights[:, :128]
                for n in range(1, len(pieces)):
                    part = part + weights[:, n * 128 : (n + 1) * 128]
                if fresh:
                    den[b, h * tok : (h + 1) * tok] = part
                else:
                    den[b, h * tok : (h + 1) * tok] += part
                rounded.append(weights.astype(bf16))
            summed = jnp.dot(jnp.concatenate(rounded, axis=0), values, preferred_element_type=f32)
            if fresh:
                acc[b] = summed
            else:
                acc[b] += summed
            if ends_plane:
                @pl.when(plane == k)
                def _():
                    for h in range(2):
                        part = slice(h * tok, (h + 1) * tok)
                        total = jnp.sum(den[b, part], axis=1, keepdims=True)
                        o_send[b, :, h * 128 : (h + 1) * 128] = (acc[b, part] / total).astype(bf16)

                    @pl.when(i < GROUP - 1)
                    def _():
                        o_copy(i).start()

            return carry

        lax.fori_loop(0, GROUP, one_block, 0)

    attend(0, (0, 1, 2, 3), True)
    for k in range(1, planes):
        @pl.when(k <= plane)
        def _(k=k):
            if k < planes - 1:
                if k > 1:
                    for d in range(GROUP):
                        from_below(k - 1, d).wait_recv()
                        send_up(k, d)
                attend(k, (0, 1, 2, 3), True)
            else:
                for pieces in ((0, 1, 2), (3,)):
                    for d in pieces:
                        if k > 1:
                            from_below(k - 1, d).wait_recv()
                    attend(k, pieces, pieces[-1] == GROUP - 1)

    load_wo.wait()
    part = y_send.shape[2]
    half = tok // 2

    def head_group(heads, group, n):
        rows = pl.ds(pl.multiple_of(group * 256, 256), 256)
        return jnp.dot(heads, wo_v[rows, n * part : (n + 1) * part], preferred_element_type=f32)

    for n in range(y_send.shape[0]):
        y_acc[n] = head_group(o_send[place], place, n)
    for i in range(GROUP - 2):
        group = (place + 2 * GROUP - 1 - i) % GROUP
        slot = o_buf.at[group]
        copy(slot, slot, o_ssem.at[i], o_rsem.at[i], peer(i + 1)).wait_recv()
        for n in range(y_send.shape[0]):
            y_acc[n] += head_group(o_buf[group], group, n)
    group = (place + 1) % GROUP
    slot = o_buf.at[group]
    copy(slot, slot, o_ssem.at[GROUP - 2], o_rsem.at[GROUP - 2], peer(GROUP - 1)).wait_recv()
    y_copies = []
    for n in range(y_send.shape[0]):
        total = y_acc[n] + head_group(o_buf[group], group, n)
        y_send[n] = jnp.where(core == 0, total[half:], total[:half]).astype(bf16)
        y_copies.append(copy(y_send.at[n], y_recv.at[n], y_ssem.at[n], y_rsem.at[n], mate))
        y_copies[n].start()
        y_mine[n] = jnp.where(core == 0, total[:half], total[half:])
    for n in range(y_send.shape[0]):
        y_copies[n].wait_recv()
        out[:, n * part : (n + 1) * part] = (y_mine[n] + y_recv[n].astype(f32)).astype(bf16)
    stores[2].start()
    for n in range(y_send.shape[0]):
        y_copies[n].wait_send()
    for d in range(1, GROUP):
        kv_copies[d].wait_send()
        q_copies[d].wait_send()
        o_copy(d - 1).wait_send()
    for k in range(planes - 1):
        @pl.when((plane < planes - 1) & (k <= plane))
        def _(k=k):
            for d in range(GROUP):
                up(k, d).wait_send()
    for store in stores:
        store.wait()


def store_kernel(a, b, c, a_out, b_out, c_out, a_held, b_held, c_held, in_sem, out_sem):
    parts = ((a, a_held, a_out), (b, b_held, b_out), (c, c_held, c_out))
    loads = [pltpu.make_async_copy(src, held, in_sem.at[n]) for n, (src, held, _) in enumerate(parts)]
    stores = [pltpu.make_async_copy(held, dst, out_sem.at[n]) for n, (_, held, dst) in enumerate(parts)]
    for load in loads:
        load.start()
    for load, store in zip(loads, stores):
        load.wait()
        store.start()
    for store in stores:
        store.wait()


def on_device_fused(hidden_in, norm_gain, w_query, w_key, w_value, w_out, q_gain, k_gain, lengths, blocks=16):
    tok, feat = hidden_in.shape
    width = w_out.shape[1]
    f32, bf16 = jnp.float32, jnp.bfloat16
    half_freq = rope_base ** (-np.arange(64, dtype=np.float64) * 2.0 / 128)
    freq = np.concatenate([half_freq, half_freq]).astype(np.float32)[None, :]
    planes = blocks // GROUP
    part = width // 5
    hbm = pl.BlockSpec(memory_space=pltpu.HBM)
    dma = pltpu.SemaphoreType.DMA
    shapes = (
        jax.ShapeDtypeStruct((tok // 2, width), bf16),
        jax.ShapeDtypeStruct((tok, w_key.shape[1]), bf16),
        jax.ShapeDtypeStruct((tok, w_value.shape[1]), bf16),
    )
    results = pl.pallas_call(
        fused_kernel,
        out_shape=shapes,
        in_specs=[hbm] * 10,
        out_specs=(hbm, hbm, hbm),
        scratch_shapes=[
            *[pltpu.VMEM(shape.shape, bf16) for shape in shapes],
            pltpu.VMEM((tok, feat), bf16),
            pltpu.VMEM((2 * feat // 128, 128), f32),
            pltpu.VMEM((1, 128), f32),
            pltpu.VMEM((1, 128), f32),
            pltpu.VMEM((1, 128), f32),
            pltpu.SMEM(lengths.shape, jnp.int32),
            pltpu.VMEM((tok, feat), bf16),
            pltpu.VMEM((2, feat, w_query.shape[1]), bf16),
            pltpu.VMEM((2, GROUP, feat, 256), bf16),
            pltpu.VMEM(w_out.shape, bf16),
            pltpu.VMEM((GROUP, tok, 256), bf16),
            pltpu.VMEM((GROUP, 2 * tok, 128), bf16),
            pltpu.VMEM((blocks, tok, 256), bf16),
            pltpu.VMEM((GROUP, 2 * tok, 128), bf16),
            pltpu.VMEM((GROUP, tok, 256), bf16),
            pltpu.VMEM((GROUP, tok, 256), bf16),
            pltpu.VMEM((GROUP, tok, 128), jnp.int32),
            pltpu.VMEM((GROUP, 2 * tok, 128), f32),
            pltpu.VMEM((GROUP, 2 * tok, 128), f32),
            pltpu.VMEM((GROUP, tok, 256), f32),
            pltpu.VMEM((5, tok, part), f32),
            pltpu.VMEM((5, tok // 2, part), bf16),
            pltpu.VMEM((5, tok // 2, part), bf16),
            pltpu.VMEM((5, tok // 2, part), f32),
            dma((6,)),
            dma((2, GROUP, 2)),
            dma((2,)),
            dma,
            dma((2,)),
            dma((GROUP,)),
            dma((GROUP,)),
            dma((GROUP,)),
            dma((GROUP,)),
            dma((planes - 1, GROUP)),
            dma((planes - 1, GROUP)),
            dma((GROUP,)),
            dma((GROUP,)),
            dma((5,)),
            dma((5,)),
            dma((3,)),
        ],
        compiler_params=pltpu.CompilerParams(
            collective_id=0, has_side_effects=True, vmem_limit_bytes=63 * 1024 * 1024
        ),
        cost_estimate=pl.CostEstimate(
            flops=3_100_000_000, bytes_accessed=17_000_000, transcendentals=2_200_000
        ),
    )(hidden_in, norm_gain.reshape(2 * feat // 128, 128), w_query, w_key, w_value, w_out,
      q_gain.reshape(1, 128), k_gain.reshape(1, 128), freq, lengths)
    return pl.pallas_call(
        store_kernel,
        out_shape=shapes,
        in_specs=[pl.BlockSpec(memory_space=pl.ANY)] * 3,
        out_specs=(hbm, hbm, hbm),
        scratch_shapes=[*[pltpu.VMEM(shape.shape, bf16) for shape in shapes], dma((3,)), dma((3,))],
        compiler_params=pltpu.CompilerParams(vmem_limit_bytes=63 * 1024 * 1024),
    )(*results)


def solution(mesh):
    seq, tensor = mesh.shape["seq"], mesh.shape["tensor"]
    fits = tensor == 2 and seq % GROUP == 0 and seq <= 16
    body = functools.partial(on_device_fused, blocks=seq) if fits else on_device
    placed = (
        P("seq", "tensor"),
        P(),
        P(None, "tensor"),
        P(None, "tensor"),
        P(None, "tensor"),
        P("tensor", None),
        P(),
        P(),
        P(),
    )
    return jax.shard_map(
        body,
        mesh=mesh,
        in_specs=placed,
        out_specs=(P(("seq", "tensor"), None), P("seq", "tensor"), P("seq", "tensor")),
        check_vma=False,
    )
```

```python
import functools
import math

import jax
import jax.numpy as jnp
import numpy as np
from jax import lax
from jax.experimental import pallas as pl
from jax.experimental.pallas import tpu as pltpu
from jax.sharding import PartitionSpec as P

rope_base = 1000000.0
norm_eps = 1e-06
masked = -1e30


def prompt_starts(lengths, token_pos):
    ends = jnp.cumsum(lengths)
    starts = ends - lengths
    before = (ends[None, :] <= token_pos[:, None]).astype(jnp.int32)
    segment = jnp.sum(before, axis=1)
    onehot = segment[:, None] == jnp.arange(lengths.shape[0], dtype=jnp.int32)[None, :]
    return jnp.sum(jnp.where(onehot, starts[None, :], 0), axis=1)


def head_norm_rope(values, gain, rel_pos):
    width = values.shape[-1]
    half = width // 2
    mean_sq = jnp.mean(values * values, axis=-1, keepdims=True)
    normed = values * lax.rsqrt(mean_sq + norm_eps) * gain
    freq = rope_base ** (-jnp.arange(half, dtype=jnp.float32) * 2.0 / width)
    angle = rel_pos.astype(jnp.float32)[:, None] * freq[None, :]
    cosine = jnp.cos(angle)[:, None, :]
    sine = jnp.sin(angle)[:, None, :]
    first = normed[..., :half]
    second = normed[..., half:]
    return jnp.concatenate(
        [first * cosine - second * sine, second * cosine + first * sine], axis=-1
    )


def on_device(hidden_in, norm_gain, w_query, w_key, w_value, w_out, q_gain, k_gain, lengths):
    tokens = hidden_in.shape[0]
    width = w_query.shape[0]
    head_dim = q_gain.shape[0]
    q_cols = w_query.shape[1]
    kv_cols = w_key.shape[1]
    kv_local = kv_cols // head_dim
    group = q_cols // kv_cols
    combined = jnp.concatenate([w_query, w_key, w_value], axis=1)
    piece = lax.all_gather(hidden_in, "tensor", axis=1, tiled=True)
    wide = piece.astype(jnp.float32)
    rows = combined
    scaled = (wide * norm_gain[None, :]).astype(jnp.bfloat16)
    acc = jnp.dot(scaled, rows, preferred_element_type=jnp.float32)
    acc, sumsq = (acc, jnp.sum(wide * wide, axis=1))
    proj = acc * lax.rsqrt(sumsq / width + norm_eps)[:, None]
    block_index = lax.axis_index("seq")
    token_pos = block_index * tokens + jnp.arange(tokens, dtype=jnp.int32)
    seg_start = prompt_starts(lengths, token_pos)
    rel_pos = token_pos - seg_start
    queries = head_norm_rope(
        proj[:, :q_cols].reshape(tokens, kv_local * group, head_dim), q_gain, rel_pos
    ).astype(jnp.bfloat16)
    keys = head_norm_rope(
        proj[:, q_cols : q_cols + kv_cols].reshape(tokens, kv_local, head_dim), k_gain, rel_pos
    ).astype(jnp.bfloat16)
    key_flat = keys.reshape(tokens, kv_cols)
    value_flat = proj[:, q_cols + kv_cols :].astype(jnp.bfloat16)
    query_grid = queries.reshape(tokens, kv_local, group, head_dim)
    inv_root = 1.0 / math.sqrt(head_dim)
    last_pos = jnp.max(token_pos)
    first_start = jnp.min(seg_start)

    def attend_block(carry, key_block, value_block, key_start):
        rows = key_block.shape[0]
        key_pos = key_start + jnp.arange(rows, dtype=jnp.int32)

        def compute(state):
            best, total, summed = state
            key_heads = key_block.reshape(rows, kv_local, head_dim)
            value_heads = value_block.reshape(rows, kv_local, head_dim)
            score = (
                jnp.einsum(
                    "qhgd,khd->hgqk", query_grid, key_heads, preferred_element_type=jnp.float32
                )
                * inv_root
            )
            visible = (key_pos[None, :] >= seg_start[:, None]) & (
                key_pos[None, :] <= token_pos[:, None]
            )
            score = jnp.where(visible[None, None], score, masked)
            fresh = jnp.maximum(best, jnp.max(score, axis=-1))
            weights = jnp.where(visible[None, None], jnp.exp(score - fresh[..., None]), 0.0)
            decay = jnp.exp(best - fresh)
            total = total * decay + jnp.sum(weights, axis=-1)
            summed = summed * decay[..., None] + jnp.einsum(
                "hgqk,khd->hgqd",
                weights.astype(jnp.bfloat16),
                value_heads,
                preferred_element_type=jnp.float32,
            )
            return (fresh, total, summed)

        seen = (key_start <= last_pos) & (key_start + rows - 1 >= first_start)
        return lax.cond(seen, compute, lambda state: state, carry)

    start_state = (
        jnp.full((kv_local, group, tokens), masked, jnp.float32),
        jnp.zeros((kv_local, group, tokens), jnp.float32),
        jnp.zeros((kv_local, group, tokens, head_dim), jnp.float32),
    )
    key_piece = lax.all_gather(key_flat, "seq", axis=0, tiled=True)
    value_piece = lax.all_gather(value_flat, "seq", axis=0, tiled=True)
    rows = key_piece.shape[0]
    size = math.gcd(rows, 512)
    count = rows // size

    def one_part(state, part):
        key_part, value_part, offset = part
        return (attend_block(state, key_part, value_part, offset), None)

    offsets = jnp.arange(count, dtype=jnp.int32) * size
    parts = (
        key_piece.reshape(count, size, kv_cols),
        value_piece.reshape(count, size, kv_cols),
        offsets,
    )
    state, unused = lax.scan(one_part, start_state, parts)
    best, total, summed = state
    attn = summed / total[..., None]
    attn = jnp.transpose(attn, (2, 0, 1, 3)).reshape(tokens, q_cols).astype(jnp.bfloat16)
    mixed = lax.psum_scatter(
        jnp.dot(attn, w_out, preferred_element_type=jnp.float32).astype(jnp.bfloat16),
        "tensor",
        scatter_dimension=0,
        tiled=True,
    )
    return (mixed, key_flat, value_flat)


GROUP = 4


def fused_kernel(
    hid_in, gain_in, wq, wk, wv, wo, q_gain_in, k_gain_in, freq_in, lens_in,
    out_hbm, key_hbm, value_hbm,
    out, key_out, value_out, hid, gain, q_gain, k_gain, freq, lens,
    peer_hid, wq_v, wkv_v, wo_v, kv_send, q_send, kv_buf, q_buf, o_send, o_buf,
    seg_q, acc, den, kv_acc, y_acc, y_send, y_recv, y_mine,
    in_sem, wkv_sem, wq_sem, wo_sem, h_sem, kv_ssem, kv_rsem, q_ssem, q_rsem,
    z_ssem, z_rsem, o_ssem, o_rsem, y_ssem, y_rsem, out_sem,
):
    f32, bf16 = jnp.float32, jnp.bfloat16
    tok, feat = hid.shape
    seq = lax.axis_index("seq")
    core = lax.axis_index("tensor")
    planes = kv_buf.shape[0] // GROUP
    plane = seq // GROUP
    place = seq % GROUP
    mate = (seq, 1 - core)
    above = (seq + GROUP, core)
    below = (seq - GROUP, core)

    def peer(d):
        return (plane * GROUP + (place + d) % GROUP, core)

    def copy(src, dst, ssem, rsem, device):
        return pltpu.make_async_remote_copy(
            src_ref=src, dst_ref=dst, send_sem=ssem, recv_sem=rsem,
            device_id=device, device_id_type=pl.DeviceIdType.MESH,
        )

    barrier = pltpu.get_barrier_semaphore()

    def greet(device):
        pl.semaphore_signal(barrier, inc=1, device_id=device, device_id_type=pl.DeviceIdType.MESH)

    greet(mate)
    for d in range(1, GROUP):
        greet(peer(d))

    @pl.when(plane < planes - 1)
    def _():
        greet(above)

    @pl.when(plane > 0)
    def _():
        greet(below)

    halves = (core, 1 - core)
    small = []
    for src, dst in (
        (hid_in, hid),
        (lens_in, lens),
        (freq_in, freq),
        (gain_in, gain),
        (q_gain_in, q_gain),
        (k_gain_in, k_gain),
    ):
        small.append(pltpu.make_async_copy(src, dst, in_sem.at[len(small)]))
        small[-1].start()

    def rows(i):
        return pl.ds(pl.multiple_of(halves[i] * feat, feat), feat)

    kv_loads, q_loads = {}, {}
    for i in range(2):
        for d in range(GROUP):
            cols = pl.ds(pl.multiple_of((place + d) % GROUP * 128, 128), 128)
            for n, w in enumerate((wk, wv)):
                kv_loads[i, d, n] = pltpu.make_async_copy(
                    w.at[rows(i), cols], wkv_v.at[i, d, :, n * 128 : (n + 1) * 128], wkv_sem.at[i, d, n]
                )
                kv_loads[i, d, n].start()
    for i in range(2):
        q_loads[i] = pltpu.make_async_copy(wq.at[rows(i)], wq_v.at[i], wq_sem.at[i])
        q_loads[i].start()
    load_wo = pltpu.make_async_copy(wo, wo_v, wo_sem)
    load_wo.start()

    for load in small:
        load.wait()

    lengths = [lens[j] for j in range(lens.shape[0])]
    ends, run = [], jnp.int32(0)
    for length in lengths:
        run = run + length
        ends.append(run)
    for b in range(GROUP):
        pos = lax.broadcasted_iota(jnp.int32, (tok, 128), 0) + (plane * GROUP + b) * tok
        start = jnp.zeros((tok, 128), jnp.int32)
        for length, end in zip(lengths, ends):
            start = start + jnp.where(end <= pos, length, 0)
        seg_q[b] = start

    neighbours = (plane + planes - 1) // planes + (2 * planes - 2 - plane) // planes
    pl.semaphore_wait(barrier, GROUP + neighbours)
    hid_copy = copy(hid, peer_hid, h_sem.at[0], h_sem.at[1], mate)
    hid_copy.start()

    def gain_row(half):
        first = half * (feat // 128)
        return jnp.concatenate([gain[pl.ds(first + r, 1)] for r in range(feat // 128)], axis=1)

    x_own = hid[...].astype(f32)
    scaled_own = (x_own * gain_row(halves[0])).astype(bf16)
    sum_own = jnp.sum(x_own * x_own, axis=1, keepdims=True)
    for d in range(GROUP):
        for n in range(2):
            kv_loads[0, d, n].wait()
    own_pos = lax.broadcasted_iota(jnp.int32, (tok, 128), 0) + seq * tok
    angle = (own_pos - seg_q[place]).astype(f32) * freq[...]
    cosine = jnp.cos(angle)
    sine = jnp.sin(angle)
    lane = lax.broadcasted_iota(jnp.int32, (tok, 128), 1)
    sine = jnp.where(lane < 64, -sine, sine)
    for d in range(GROUP):
        kv_acc[d] = jnp.dot(scaled_own, wkv_v[0, d], preferred_element_type=f32)

    def q_cols(d):
        return pl.ds(pl.multiple_of((place + d) % GROUP * 256, 256), 256)

    hid_copy.wait()
    x_far = peer_hid[...].astype(f32)
    scaled_far = (x_far * gain_row(halves[1])).astype(bf16)
    sumsq = sum_own + jnp.sum(x_far * x_far, axis=1, keepdims=True)
    inv = lax.rsqrt(sumsq / (2 * feat) + norm_eps)

    def rope(u, g):
        u = u * lax.rsqrt(jnp.mean(u * u, axis=1, keepdims=True) + norm_eps) * g[...]
        return (u * cosine + pltpu.roll(u, 64, 1) * sine).astype(bf16)

    def up(k, d):
        slot = kv_buf.at[(plane - k) * GROUP + (place + GROUP - d) % GROUP]
        return copy(slot, slot, z_ssem.at[k, d], z_rsem.at[k, d], above)

    def from_below(k, d):
        slot = kv_buf.at[(plane - 1 - k) * GROUP + (place + GROUP - d) % GROUP]
        return copy(slot, slot, z_ssem.at[k, d], z_rsem.at[k, d], below)

    def send_up(k, d):
        @pl.when(plane < planes - 1)
        def _():
            up(k, d).start()

    kv_copies, q_copies = {}, {}
    for d in range(GROUP):
        for n in range(2):
            kv_loads[1, d, n].wait()
        pair = kv_acc[d] + jnp.dot(scaled_far, wkv_v[1, d], preferred_element_type=f32)
        pair = pair * inv
        key = rope(pair[:, :128], k_gain)
        value = pair[:, 128:].astype(bf16)
        cols = pl.ds(pl.multiple_of((place + d) % GROUP * 128, 128), 128)
        key_out[:, cols] = key
        value_out[:, cols] = value
        if d == 0:
            kv_buf[seq, :, :128] = key
            kv_buf[seq, :, 128:] = value
            send_up(0, 0)
        else:
            kv_send[d, :, :128] = key
            kv_send[d, :, 128:] = value
            kv_copies[d] = copy(kv_send.at[d], kv_buf.at[seq], kv_ssem.at[d], kv_rsem.at[d], peer(d))
            kv_copies[d].start()

    stores = [
        pltpu.make_async_copy(src, dst, out_sem.at[n])
        for n, (src, dst) in enumerate(((key_out, key_hbm), (value_out, value_hbm), (out, out_hbm)))
    ]
    stores[0].start()
    stores[1].start()

    def kv_arrival(d):
        slot = kv_buf.at[plane * GROUP + (place + GROUP - d) % GROUP]
        return copy(slot, slot, kv_ssem.at[d], kv_rsem.at[d], peer(d))

    q_loads[0].wait()
    q_loads[1].wait()
    for turn, d in enumerate((1, 2, 3, 0)):
        pair = jnp.dot(scaled_own, wq_v[0, :, q_cols(d)], preferred_element_type=f32)
        pair = pair + jnp.dot(scaled_far, wq_v[1, :, q_cols(d)], preferred_element_type=f32)
        pair = pair * inv
        for i in range(2):
            query = rope(pair[:, i * 128 : (i + 1) * 128], q_gain)
            if d == 0:
                q_buf[place, i * tok : (i + 1) * tok] = query
            else:
                q_send[d, i * tok : (i + 1) * tok] = query
        if d > 0:
            q_copies[d] = copy(q_send.at[d], q_buf.at[place], q_ssem.at[d], q_rsem.at[d], peer(d))
            q_copies[d].start()
        if turn == 0:
            @pl.when(plane >= 1)
            def _():
                from_below(0, 0).wait_recv()
                send_up(1, 0)

        if turn < GROUP - 1:
            kv_arrival(turn + 1).wait_recv()
            send_up(0, turn + 1)

    @pl.when(plane >= 1)
    def _():
        for d in range(1, GROUP):
            from_below(0, d).wait_recv()
            send_up(1, d)

    for d in range(1, GROUP):
        slot = q_buf.at[(place + GROUP - d) % GROUP]
        copy(slot, slot, q_ssem.at[d], q_rsem.at[d], peer(d)).wait_recv()

    scale = math.log2(math.e) / math.sqrt(128)

    def o_copy(i):
        b = (place + 1 + i) % GROUP
        return copy(o_send.at[b], o_buf.at[place], o_ssem.at[i], o_rsem.at[i], (plane * GROUP + b, core))

    def attend(k, pieces, ends_plane):
        slots = [(plane - k) * GROUP + (place + GROUP - d) % GROUP for d in pieces]
        span = 128 * len(pieces)
        lanes = lax.broadcasted_iota(jnp.int32, (tok, 128), 1)
        key_pos = jnp.concatenate([lanes + slot * tok for slot in slots], axis=1)
        fresh = k == 0 and pieces[0] == 0

        def one_block(i, carry):
            b = (place + 1 + i) % GROUP
            keys = jnp.concatenate([kv_buf[slot, :, :128] for slot in slots], axis=0)
            values = jnp.concatenate([kv_buf[slot, :, 128:] for slot in slots], axis=0)
            start = jnp.concatenate([seg_q[b]] * len(pieces), axis=1)
            visible = key_pos >= start
            if k == 0:
                q_pos = lax.broadcasted_iota(jnp.int32, (tok, span), 0) + (plane * GROUP + b) * tok
                visible = visible & (key_pos <= q_pos)
            score = lax.dot_general(
                q_buf[b], keys, (((1,), (1,)), ((), ())), preferred_element_type=f32
            )
            rounded = []
            for h in range(2):
                weights = jnp.where(visible, jnp.exp2(score[h * tok : (h + 1) * tok] * scale), 0.0)
                part = weights[:, :128]
                for n in range(1, len(pieces)):
                    part = part + weights[:, n * 128 : (n + 1) * 128]
                if fresh:
                    den[b, h * tok : (h + 1) * tok] = part
                else:
                    den[b, h * tok : (h + 1) * tok] += part
                rounded.append(weights.astype(bf16))
            summed = jnp.dot(jnp.concatenate(rounded, axis=0), values, preferred_element_type=f32)
            if fresh:
                acc[b] = summed
            else:
                acc[b] += summed
            if ends_plane:
                @pl.when(plane == k)
                def _():
                    for h in range(2):
                        part = slice(h * tok, (h + 1) * tok)
                        total = jnp.sum(den[b, part], axis=1, keepdims=True)
                        o_send[b, :, h * 128 : (h + 1) * 128] = (acc[b, part] / total).astype(bf16)

                    @pl.when(i < GROUP - 1)
                    def _():
                        o_copy(i).start()

            return carry

        lax.fori_loop(0, GROUP, one_block, 0)

    attend(0, (0, 1, 2, 3), True)
    for k in range(1, planes):
        @pl.when(k <= plane)
        def _(k=k):
            if k < planes - 1:
                if k > 1:
                    for d in range(GROUP):
                        from_below(k - 1, d).wait_recv()
                        send_up(k, d)
                attend(k, (0, 1, 2, 3), True)
            else:
                for pieces in ((0, 1, 2), (3,)):
                    for d in pieces:
                        if k > 1:
                            from_below(k - 1, d).wait_recv()
                    attend(k, pieces, pieces[-1] == GROUP - 1)

    load_wo.wait()
    part = y_send.shape[2]
    half = tok // 2

    def head_group(heads, group, n):
        rows = pl.ds(pl.multiple_of(group * 256, 256), 256)
        return jnp.dot(heads, wo_v[rows, n * part : (n + 1) * part], preferred_element_type=f32)

    for n in range(y_send.shape[0]):
        y_acc[n] = head_group(o_send[place], place, n)
    for i in range(GROUP - 2):
        group = (place + 2 * GROUP - 1 - i) % GROUP
        slot = o_buf.at[group]
        copy(slot, slot, o_ssem.at[i], o_rsem.at[i], peer(i + 1)).wait_recv()
        for n in range(y_send.shape[0]):
            y_acc[n] += head_group(o_buf[group], group, n)
    group = (place + 1) % GROUP
    slot = o_buf.at[group]
    copy(slot, slot, o_ssem.at[GROUP - 2], o_rsem.at[GROUP - 2], peer(GROUP - 1)).wait_recv()
    y_copies = []
    for n in range(y_send.shape[0]):
        total = y_acc[n] + head_group(o_buf[group], group, n)
        y_send[n] = jnp.where(core == 0, total[half:], total[:half]).astype(bf16)
        y_copies.append(copy(y_send.at[n], y_recv.at[n], y_ssem.at[n], y_rsem.at[n], mate))
        y_copies[n].start()
        y_mine[n] = jnp.where(core == 0, total[:half], total[half:])
    for n in range(y_send.shape[0]):
        y_copies[n].wait_recv()
        out[:, n * part : (n + 1) * part] = (y_mine[n] + y_recv[n].astype(f32)).astype(bf16)
    stores[2].start()
    for n in range(y_send.shape[0]):
        y_copies[n].wait_send()
    for d in range(1, GROUP):
        kv_copies[d].wait_send()
        q_copies[d].wait_send()
        o_copy(d - 1).wait_send()
    for k in range(planes - 1):
        @pl.when((plane < planes - 1) & (k <= plane))
        def _(k=k):
            for d in range(GROUP):
                up(k, d).wait_send()
    for store in stores:
        store.wait()


def store_kernel(a, b, c, a_out, b_out, c_out, a_held, b_held, c_held, in_sem, out_sem):
    parts = ((a, a_held, a_out), (b, b_held, b_out), (c, c_held, c_out))
    loads = [pltpu.make_async_copy(src, held, in_sem.at[n]) for n, (src, held, _) in enumerate(parts)]
    stores = [pltpu.make_async_copy(held, dst, out_sem.at[n]) for n, (_, held, dst) in enumerate(parts)]
    for load in loads:
        load.start()
    for load, store in zip(loads, stores):
        load.wait()
        store.start()
    for store in stores:
        store.wait()


def on_device_fused(hidden_in, norm_gain, w_query, w_key, w_value, w_out, q_gain, k_gain, lengths, blocks=16):
    tok, feat = hidden_in.shape
    width = w_out.shape[1]
    f32, bf16 = jnp.float32, jnp.bfloat16
    half_freq = rope_base ** (-np.arange(64, dtype=np.float64) * 2.0 / 128)
    freq = np.concatenate([half_freq, half_freq]).astype(np.float32)[None, :]
    planes = blocks // GROUP
    part = width // 5
    hbm = pl.BlockSpec(memory_space=pltpu.HBM)
    dma = pltpu.SemaphoreType.DMA
    shapes = (
        jax.ShapeDtypeStruct((tok // 2, width), bf16),
        jax.ShapeDtypeStruct((tok, w_key.shape[1]), bf16),
        jax.ShapeDtypeStruct((tok, w_value.shape[1]), bf16),
    )
    results = pl.pallas_call(
        fused_kernel,
        out_shape=shapes,
        in_specs=[hbm] * 10,
        out_specs=(hbm, hbm, hbm),
        scratch_shapes=[
            *[pltpu.VMEM(shape.shape, bf16) for shape in shapes],
            pltpu.VMEM((tok, feat), bf16),
            pltpu.VMEM((2 * feat // 128, 128), f32),
            pltpu.VMEM((1, 128), f32),
            pltpu.VMEM((1, 128), f32),
            pltpu.VMEM((1, 128), f32),
            pltpu.SMEM(lengths.shape, jnp.int32),
            pltpu.VMEM((tok, feat), bf16),
            pltpu.VMEM((2, feat, w_query.shape[1]), bf16),
            pltpu.VMEM((2, GROUP, feat, 256), bf16),
            pltpu.VMEM(w_out.shape, bf16),
            pltpu.VMEM((GROUP, tok, 256), bf16),
            pltpu.VMEM((GROUP, 2 * tok, 128), bf16),
            pltpu.VMEM((blocks, tok, 256), bf16),
            pltpu.VMEM((GROUP, 2 * tok, 128), bf16),
            pltpu.VMEM((GROUP, tok, 256), bf16),
            pltpu.VMEM((GROUP, tok, 256), bf16),
            pltpu.VMEM((GROUP, tok, 128), jnp.int32),
            pltpu.VMEM((GROUP, 2 * tok, 128), f32),
            pltpu.VMEM((GROUP, 2 * tok, 128), f32),
            pltpu.VMEM((GROUP, tok, 256), f32),
            pltpu.VMEM((5, tok, part), f32),
            pltpu.VMEM((5, tok // 2, part), bf16),
            pltpu.VMEM((5, tok // 2, part), bf16),
            pltpu.VMEM((5, tok // 2, part), f32),
            dma((6,)),
            dma((2, GROUP, 2)),
            dma((2,)),
            dma,
            dma((2,)),
            dma((GROUP,)),
            dma((GROUP,)),
            dma((GROUP,)),
            dma((GROUP,)),
            dma((planes - 1, GROUP)),
            dma((planes - 1, GROUP)),
            dma((GROUP,)),
            dma((GROUP,)),
            dma((5,)),
            dma((5,)),
            dma((3,)),
        ],
        compiler_params=pltpu.CompilerParams(
            collective_id=0, has_side_effects=True, vmem_limit_bytes=63 * 1024 * 1024
        ),
        cost_estimate=pl.CostEstimate(
            flops=3_100_000_000, bytes_accessed=17_000_000, transcendentals=2_200_000
        ),
    )(hidden_in, norm_gain.reshape(2 * feat // 128, 128), w_query, w_key, w_value, w_out,
      q_gain.reshape(1, 128), k_gain.reshape(1, 128), freq, lengths)
    return pl.pallas_call(
        store_kernel,
        out_shape=shapes,
        in_specs=[pl.BlockSpec(memory_space=pl.ANY)] * 3,
        out_specs=(hbm, hbm, hbm),
        scratch_shapes=[*[pltpu.VMEM(shape.shape, bf16) for shape in shapes], dma((3,)), dma((3,))],
        compiler_params=pltpu.CompilerParams(vmem_limit_bytes=63 * 1024 * 1024),
    )(*results)


def solution(mesh):
    seq, tensor = mesh.shape["seq"], mesh.shape["tensor"]
    fits = tensor == 2 and seq % GROUP == 0 and seq <= 16
    body = functools.partial(on_device_fused, blocks=seq) if fits else on_device
    placed = (
        P("seq", "tensor"),
        P(),
        P(None, "tensor"),
        P(None, "tensor"),
        P(None, "tensor"),
        P("tensor", None),
        P(),
        P(),
        P(),
    )
    return jax.shard_map(
        body,
        mesh=mesh,
        in_specs=placed,
        out_specs=(P(("seq", "tensor"), None), P("seq", "tensor"), P("seq", "tensor")),
        check_vma=False,
    )
```
